256 devices in a mesh: group: 2 (over core), seq: 16 (over y, x), expert: 8 (over z).
Axes of the slice: x: 4, y: 4, z: 8, core: 2. Of those that a mesh axis runs over, the one named last changes fastest.
Arguments:
- q_pre: bfloat16 [2, 2048, 36864], P('group', 'seq', 'expert'), may hold values from -48 to 48
- prefix_cache: bfloat16 [2, 576, 2048], P('group', None, 'seq'), may hold values from -6 to 6
- span_cache: bfloat16 [2, 576, 2048], P('group', None, 'seq'), may hold values from -6 to 6
- prefix_len: int32 [2], P('group'), may hold values from 1 to 2048, as said below
- q_dec: bfloat16 [256, 36864], P(('group', 'seq'), 'expert'), may hold values from -48 to 48
- dec_cache: bfloat16 [256, 576, 128], P(('group', 'seq')), may hold values from -6 to 6
- cache_len: int32 [256], P(('group', 'seq')), may hold values from 1 to 128, as said below
- requests: int32 [256], P(('group', 'seq')), may hold values from 0 to 2
- w_uv: bfloat16 [64, 512, 128], P('expert'), may hold values from -0.25 to 0.25
- w_out: bfloat16 [8192, 7168], P('expert', 'seq'), may hold values from -0.0625 to 0.0625
- x_dec: bfloat16 [256, 7168], P(('group', 'expert'), 'seq'), may hold values from -3 to 3
- norm_gain: float32 [7168], replicated, may hold values from 0.5 to 1.5
- expert_ids: int32 [256, 8], P(('group', 'expert')), may hold values from 0 to 15, all different within a row; in each aligned block of 16 rows (0 to 15, 16 to 31, ...) at most 12 rows name the same one
- expert_gates: float32 [256, 8], P(('group', 'expert')), may hold values from 0.1 to 1
- w_in: bfloat16 [16, 2, 7168, 2048], P(('group', 'expert'), None, None, 'seq'), may hold values from -0.0625 to 0.0625
- w_down: bfloat16 [16, 2048, 7168], P(('group', 'expert'), 'seq'), may hold values from -0.125 to 0.125
Outputs:
- o_pre: bfloat16 [2, 2048, 32768], P('group', 'seq', 'expert')
- h_out: bfloat16 [256, 7168], P(('group', 'expert'), 'seq')
The draws below stay inside these ranges and needn't reach their ends.
Inputs may be any that keep to these rules, and one draw needn't show every extreme that they name: `prefix_len`: the first prompt has all 2048 earlier columns valid. `cache_len`: every eighth decode row has all 128 resident columns valid. `expert_ids`: A row names 8 different experts; among the 16 rows of one aligned block no expert is named more than 12 times.
All inputs are finite; a program needn't handle non-finite values.
Results may differ from the reference program's by a relative error of at most 0.029.
Values may be sent and summed in bfloat16 or wider, within the bound.
No kernel may reach another device: no remote copies, remote signals or barrier semaphores. Data moves between devices by JAX's collectives and lax.ppermute only.
A program may use at most 192 MiB of HBM per device.

```python
import math
import jax
import jax.numpy as jnp
import numpy as np
from jax import lax

D = 7168
FF = 2048
LATENT = 512
VDIM = 128
TOPK = 8
HEADS = 64
CTX = 128
KVW = 576
SPAN = 2048
PREFIX = 2048
PROMPTS = 2
ROWS = 256
BLOCK = 16
EXPERTS = 16
CAP = 12


def prompt_columns(key):
    return jnp.clip(jax.random.normal(jax.random.fold_in(key, 11), (PROMPTS, KVW, PREFIX), jnp.float32), -6.0, 6.0)


def row_columns(key):
    return jnp.clip(jax.random.normal(jax.random.fold_in(key, 13), (ROWS, KVW, CTX), jnp.float32), -6.0, 6.0)


def draw_prefix_cache(key, part):
    shared = prompt_columns(key)
    return shared.astype(jnp.bfloat16)


def draw_q_pre(key, part):
    key = jax.random.fold_in(key, 5)
    queries = jnp.clip(jax.random.normal(key, (PROMPTS, SPAN, HEADS, KVW), jnp.float32), -6.0, 6.0)
    return queries.reshape(PROMPTS, SPAN, HEADS * KVW).astype(jnp.bfloat16)


def draw_dec_cache(key, part):
    shared = row_columns(key)
    return shared.astype(jnp.bfloat16)


def draw_q_dec(key, part):
    key = jax.random.fold_in(key, 7)
    queries = jnp.clip(jax.random.normal(key, (ROWS, HEADS, KVW), jnp.float32), -6.0, 6.0)
    return queries.reshape(ROWS, HEADS * KVW).astype(jnp.bfloat16)


def draw_prefix_len(key, part):
    key = jax.random.fold_in(key, 17)
    drawn = jax.random.randint(key, (PROMPTS,), 1, PREFIX + 1)
    return jnp.where(jnp.arange(PROMPTS) == 0, PREFIX, drawn).astype(jnp.int32)


def draw_cache_len(key, part):
    key = jax.random.fold_in(key, 19)
    drawn = jax.random.randint(key, (ROWS,), 1, CTX + 1)
    return jnp.where(jnp.arange(ROWS) % 8 == 0, CTX, drawn).astype(jnp.int32)


def with_ends(values, rng, low, high):
    dims = values.shape
    index_at = [jax.random.randint(jax.random.fold_in(rng, axis), (), 0, dims[axis]) for axis in range(len(dims))]
    values = values.at[tuple(index_at)].set(low)
    longest = dims.index(max(dims))
    index_at[longest] = (index_at[longest] + 1) % dims[longest]
    return values.at[tuple(index_at)].set(high)


def steps_of(stream_key, extent, pieces, low, largest):
    factor_of = 1.0
    for position, blocks in pieces:
        heights = jax.random.uniform(jax.random.fold_in(jax.random.fold_in(stream_key, 6), position), (blocks,), jnp.float32, low / len(pieces), largest / len(pieces))
        factor_of = factor_of * jnp.repeat(jnp.exp(heights), extent[position] // blocks).reshape((-1,) + (1,) * (len(extent) - 1 - position))
    return factor_of


def assign_block(key, own, number, rows, count, top, bound, slope):
    order = jax.random.permutation(key, count)
    packed, usual = load_shares(count, rows * top, bound, slope, True), load_shares(count, rows * top, bound, slope, False)
    places = jnp.arange(count)

    def named(tallies, rotation):
        used = int((tallies > 0).sum())
        fixed = max(1, used // 4)
        moved = fixed + (places - fixed + rotation * (used - fixed)) % max(1, count - fixed)
        return jnp.zeros((count,), jnp.int32).at[order[jnp.where(places < fixed, places, moved)]].set(jnp.asarray(tallies, jnp.int32))

    tallies = jnp.where(number % 4 == 0, named(packed, number // 4), named(usual, number - number // 4 - 1))
    mixed = jax.random.permutation(jax.random.fold_in(own, 3), count)
    giver, sink = mixed[0:count // 2 * 2:2], mixed[1:count // 2 * 2:2]
    room = jnp.minimum(tallies[giver] - 1, bound - tallies[sink]) // 2
    room = jnp.where((giver == order[0]) | (sink == order[0]) | (tallies[sink] == 0), 0, jnp.maximum(room, 0))
    moved = jax.random.randint(jax.random.fold_in(own, 4), (count // 2,), 0, 1 << 20) % (room + 1)
    tallies = tallies.at[giver].add(-moved).at[sink].add(moved)
    members = jnp.searchsorted(jnp.cumsum(tallies), jnp.arange(rows * top), side="right").astype(jnp.int32)
    listing = members.reshape(top, rows).T
    listing = listing[jax.random.permutation(jax.random.fold_in(own, 1), rows)]
    rotation = jax.random.randint(jax.random.fold_in(own, 2), (rows, 1), 0, top)
    return jnp.take_along_axis(listing, (jnp.arange(top)[None, :] + rotation) % top, axis=1)


def load_shares(amount, total, bound, skew, full):
    loads = [(1 << 20) // math.isqrt(grade ** skew) + 1 for grade in range(1, amount + 1)]
    largest = bound if full else min(bound, max(-(-total // amount), total * loads[0] // sum(loads)))
    least = 1 if total - largest >= amount - 1 else 0
    given, spare = [largest] + [least] * (amount - 1), total - largest - least * (amount - 1)
    while spare > 0:
        movable = [i for i in range(1, amount) if given[i] < largest] or [i for i in range(1, amount) if given[i] < bound]
        whole, remaining = sum([loads[i] for i in movable]), spare
        for i in movable:
            extra = min(bound - given[i], max(1, remaining * loads[i] // whole), spare)
            given[i] = given[i] + extra
            spare = spare - extra
    return np.array(given)


def gaussian(stream_key, shape, spread, most, shards=(), kind=jnp.bfloat16):
    values = spread * jax.random.normal(stream_key, shape, jnp.float32)
    if shards:
        values = values * steps_of(stream_key, shape, shards, -0.22, 0.18)
    return jnp.clip(values, -most, most).astype(kind)


def setup_inputs(seed: int = 0) -> dict:
    key_of = jax.random.split(jax.random.key(seed), 17)
    q_pre = draw_q_pre(jax.random.fold_in(key_of[16], 71), 0)
    prefix_cache = draw_prefix_cache(jax.random.fold_in(key_of[16], 71), 0)
    span_cache = gaussian(key_of[2], (PROMPTS, KVW, SPAN), 1.0, 6.0, ((0, 2), (2, 16)))
    prefix_len = draw_prefix_len(jax.random.fold_in(key_of[16], 71), 0)
    q_dec = draw_q_dec(jax.random.fold_in(key_of[16], 71), 0)
    dec_cache = draw_dec_cache(jax.random.fold_in(key_of[16], 71), 0)
    cache_len = draw_cache_len(jax.random.fold_in(key_of[16], 71), 0)
    requests = with_ends(jax.random.randint(key_of[7], (ROWS,), 0, PROMPTS + 1), jax.random.fold_in(key_of[7], 1), 0, PROMPTS).astype(jnp.int32)
    w_uv = gaussian(key_of[8], (HEADS, LATENT, VDIM), LATENT ** -0.5, 0.25, ((0, 8),))
    w_out = gaussian(key_of[9], (HEADS * VDIM, D), (HEADS * VDIM) ** -0.5, 0.0625, ((0, 8), (1, 16)))
    x_dec = gaussian(key_of[10], (ROWS, D), 0.5, 3.0, ((0, 16), (1, 16)))
    norm_gain = jnp.clip(1.0 + 0.1 * jax.random.normal(key_of[11], (D,), jnp.float32), 0.5, 1.5)
    expert_ids_keys = jax.random.split(jax.random.fold_in(key_of[12], 1), ROWS // BLOCK)
    expert_ids_turns = jax.random.permutation(jax.random.fold_in(key_of[12], 3), ROWS // BLOCK)
    expert_ids = jax.vmap(lambda own, number: assign_block(jax.random.fold_in(key_of[12], 2), own, number, BLOCK, EXPERTS, TOPK, CAP, 2))(expert_ids_keys, expert_ids_turns).reshape((ROWS, TOPK))
    expert_gates = jnp.clip(jnp.exp(math.log(1.0) - 2.3025851 * jax.random.uniform(key_of[13], (ROWS, TOPK), jnp.float32) ** steps_of(key_of[13], (ROWS, TOPK), ((0, 16),), -0.2, 0.2)), 0.1, 1.0)
    w_in = gaussian(key_of[14], (EXPERTS, 2, D, FF), D ** -0.5, 0.0625, ((0, 16), (3, 16)))
    w_down = gaussian(key_of[15], (EXPERTS, FF, D), FF ** -0.5, 0.125, ((0, 16), (1, 16)))
    return dict(q_pre=q_pre, prefix_cache=prefix_cache, span_cache=span_cache, prefix_len=prefix_len, q_dec=q_dec, dec_cache=dec_cache, cache_len=cache_len, requests=requests, w_uv=w_uv, w_out=w_out, x_dec=x_dec, norm_gain=norm_gain, expert_ids=expert_ids, expert_gates=expert_gates, w_in=w_in, w_down=w_down)


score_scale = 192.0 ** (-0.5)
epsilon = 1e-06

def attend(queries, keys, valid):
    scores = jnp.dot(queries, keys, preferred_element_type=jnp.float32) * score_scale
    scores = jnp.where(valid, scores, -jnp.inf)
    highest = lax.optimization_barrier(jnp.max(scores, axis=1, keepdims=True))
    expd = jnp.where(valid, jnp.exp(scores - highest), 0.0)
    total = lax.optimization_barrier(jnp.sum(expd, axis=1, keepdims=True))
    weighted = lax.dot_general(expd.astype(jnp.bfloat16), keys[:LATENT], (((1,), (1,)), ((), ())), preferred_element_type=jnp.float32)
    return (weighted / total).astype(jnp.bfloat16)

def reference(q_pre, prefix_cache, span_cache, prefix_len, q_dec, dec_cache, cache_len, requests, w_uv, w_out, x_dec, norm_gain, expert_ids, expert_gates, w_in, w_down):
    column = jnp.arange(SPAN, dtype=jnp.int32)
    earlier = jnp.arange(PREFIX, dtype=jnp.int32)
    outputs = []
    for prompt in range(PROMPTS):
        keys = jnp.concatenate([prefix_cache[prompt], span_cache[prompt]], axis=1)
        valid = jnp.concatenate([jnp.broadcast_to(earlier[None, :] < prefix_len[prompt], (SPAN, PREFIX)), column[None, :] <= column[:, None]], axis=1)
        queries = jnp.moveaxis(q_pre[prompt].reshape(SPAN, HEADS, KVW), 1, 0)
        heads_out = lax.map(lambda single: attend(single, keys, valid), queries)
        outputs.append(jnp.moveaxis(heads_out, 0, 1).reshape(SPAN, HEADS * LATENT))
    o_pre = jnp.stack(outputs)
    context = jnp.arange(CTX, dtype=jnp.int32)

    def decode_row(item):
        query, cache, length, request = item
        chosen = jnp.clip(request, 0, PROMPTS - 1).astype(jnp.int32)
        span_keys = lax.dynamic_index_in_dim(span_cache, chosen, 0, keepdims=False)
        keys = jnp.concatenate([cache, span_keys], axis=1)
        valid = jnp.concatenate([context < length, jnp.broadcast_to(request < PROMPTS, (SPAN,))])[None, :]
        return attend(query.reshape(HEADS, KVW), keys, valid)
    dec_lat = lax.map(decode_row, (q_dec, dec_cache, cache_len, requests))
    dec_val = jnp.einsum('rhl,hlv->rhv', dec_lat.astype(jnp.float32), w_uv.astype(jnp.float32)).astype(jnp.bfloat16).reshape(ROWS, HEADS * VDIM)
    hidden = (x_dec.astype(jnp.float32) + jnp.dot(dec_val, w_out, preferred_element_type=jnp.float32)).astype(jnp.bfloat16)
    wide = hidden.astype(jnp.float32)
    normed = (wide * lax.rsqrt(lax.optimization_barrier(jnp.mean(wide * wide, axis=1, keepdims=True)) + epsilon) * norm_gain).astype(jnp.bfloat16)
    chosen_mask = expert_ids[:, :, None] == jnp.arange(EXPERTS, dtype=jnp.int32)[None, None, :]
    route = lax.optimization_barrier(jnp.sum(jnp.where(chosen_mask, expert_gates[:, :, None], 0.0), axis=1))

    def one_expert(total, item):
        w_pair, w_back, weight = item
        gate = jnp.dot(normed, w_pair[0], preferred_element_type=jnp.float32)
        upper = jnp.dot(normed, w_pair[1], preferred_element_type=jnp.float32)
        act = (jax.nn.silu(gate) * upper).astype(jnp.bfloat16)
        result = jnp.dot(act, w_back, preferred_element_type=jnp.float32)
        return (total + weight[:, None] * result, None)
    moe, unused = lax.scan(one_expert, jnp.zeros((ROWS, D), jnp.float32), (w_in, w_down, route.T))
    h_out = (wide + moe).astype(jnp.bfloat16)
    return (o_pre, h_out)
```

```python
import functools

import jax
import jax.numpy as jnp
from jax import lax
from jax.experimental import pallas as pl
from jax.experimental.pallas import tpu as pltpu
from jax.sharding import PartitionSpec as P

LATENT = 512
VDIM = 128
SIDE = 4
CAP = 12

bf16 = jnp.bfloat16
f32 = jnp.float32
score_scale = 192.0 ** (-0.5)
epsilon = 1e-06
LOW = -1e30

VMEM = pl.BlockSpec(memory_space=pltpu.VMEM)
SMEM = pl.BlockSpec(memory_space=pltpu.SMEM)


def call(kernel, out_shape, ins, scratch=(), cost=None, limit=48 << 20):
    multi = isinstance(out_shape, (tuple, list))
    return pl.pallas_call(
        kernel,
        out_shape=out_shape,
        in_specs=[SMEM] + [VMEM] * (len(ins) - 1),
        out_specs=[VMEM] * len(out_shape) if multi else VMEM,
        scratch_shapes=list(scratch),
        compiler_params=pltpu.CompilerParams(vmem_limit_bytes=limit),
        cost_estimate=cost,
    )(*ins)


def nn(a, b):
    return jnp.dot(a, b, preferred_element_type=f32)


def nt(a, b):
    return lax.dot_general(a, b, (((1,), (1,)), ((), ())), preferred_element_type=f32)


def tn(a, b):
    return lax.dot_general(a, b, (((0,), (0,)), ((), ())), preferred_element_type=f32)


def split3(v):
    high = v.astype(bf16).astype(f32)
    rest = v - high
    mid = rest.astype(bf16).astype(f32)
    return high, mid, (rest - mid).astype(bf16).astype(f32)


def along_x(array):
    return [array] + [
        lax.ppermute(
            array,
            "seq",
            [(y * SIDE + x, y * SIDE + (x + d) % SIDE) for y in range(SIDE) for x in range(SIDE)],
        )
        for d in range(1, SIDE)
    ]


def along_y(array):
    return [array] + [
        lax.ppermute(
            array,
            "seq",
            [(y * SIDE + x, (y + d) % SIDE * SIDE + x) for y in range(SIDE) for x in range(SIDE)],
        )
        for d in range(1, SIDE)
    ]


def other_core(array):
    return lax.ppermute(array, "group", [(0, 1), (1, 0)])


def everyone(array, axis, count):
    return lax.all_to_all(
        jnp.broadcast_to(array[None], (count,) + array.shape), axis, 0, 0, tiled=True
    )


def resident_kernel(lens, q_ref, cache_ref, m_ref, l_ref, w_ref):
    count = cache_ref.shape[0]
    queries = q_ref[:, :576]
    row = lax.rem(lax.broadcasted_iota(jnp.int32, (queries.shape[0], 128), 0), count)
    column = lax.broadcasted_iota(jnp.int32, (queries.shape[0], 128), 1)
    scores = []
    for r in range(count):
        s = nn(queries, cache_ref[r]) * score_scale
        scores.append(jnp.where((row == r) & (column < lens[r]), s, LOW))
    top = scores[0]
    for s in scores[1:]:
        top = jnp.maximum(top, s)
    m = jnp.max(top, axis=1, keepdims=True)
    total = jnp.zeros_like(top)
    weighted = jnp.zeros((queries.shape[0], LATENT), f32)
    for r in range(count):
        p = jnp.where((row == r) & (column < lens[r]), jnp.exp(scores[r] - m), 0.0)
        total += p
        weighted += nt(p.astype(bf16), cache_ref[r, :LATENT])
    m_ref[...] = m
    l_ref[...] = jnp.sum(total, axis=1, keepdims=True)
    w_ref[...] = weighted


def span_kernel(
    info, q0, q1, q2, q3, k0, k1, k2, k3, kp, w_uv, rm, rl, rw, out_ref, scr
):
    group = info[0].astype(f32)
    y = info[1]
    packed = jnp.concatenate([q0[...], q1[...], q2[...], q3[...]], axis=0)
    queries = packed[:, :576]
    wanted = packed[:, 576:577].astype(f32)
    own_keys = jnp.concatenate([k0[...], k1[...], k2[...], k3[...]], axis=1)
    far_keys = jnp.concatenate([kp[0], kp[1], kp[2], kp[3]], axis=1)
    own = wanted == group
    valid = wanted < 1.5
    s = jnp.where(own, nn(queries, own_keys), nn(queries, far_keys)) * score_scale
    m = jnp.where(valid, jnp.max(s, axis=1, keepdims=True), LOW)
    p = jnp.where(valid, jnp.exp(s - m), 0.0)
    total = jnp.sum(p, axis=1, keepdims=True)
    weighted = nt(jnp.where(own, p, 0.0).astype(bf16), own_keys[:LATENT]) + nt(
        jnp.where(own, 0.0, p).astype(bf16), far_keys[:LATENT]
    )
    here = q0.shape[0]
    newest = jnp.maximum(m[:here], rm[...])
    a = jnp.exp(m[:here] - newest)
    b = jnp.exp(rm[...] - newest)
    m = jnp.concatenate([newest, m[here:]], axis=0)
    total = jnp.concatenate([total[:here] * a + rl[...] * b, total[here:]], axis=0)
    weighted = jnp.concatenate([weighted[:here] * a + rw[...] * b, weighted[here:]], axis=0)
    some = total > 0.0
    safe = jnp.where(some, total, 1.0)
    latent = (weighted / safe).reshape(SIDE, 8, 8, LATENT)
    level = jnp.where(some, m + jnp.log(safe), LOW).reshape(SIDE, 8, 8, 1)
    lane = lax.broadcasted_iota(jnp.int32, (SIDE, 8, 128), 2)
    tail = jnp.zeros((SIDE, 8, 128), f32)
    places = [lax.rem(y - d + SIDE, SIDE) for d in range(SIDE)]
    for h in range(8):
        rows = latent[:, h].reshape(SIDE * 8, LATENT).astype(bf16)
        value = nn(rows, w_uv[h])
        for d in range(SIDE):
            scr[places[d], :, h * VDIM : (h + 1) * VDIM] = value[d * 8 : (d + 1) * 8]
        for part, v in enumerate(split3(level[:, h])):
            tail = jnp.where(lane == part * 8 + h, v, tail)
    for d in range(SIDE):
        scr[places[d], :, 8 * VDIM :] = tail[d]
    out_ref[...] = scr[...].reshape(SIDE * 8, 9 * VDIM).astype(bf16)


def merge_kernel(info, p0, p1, p2, p3, out_ref):
    parts = [p0, p1, p2, p3]
    levels = []
    for p in parts:
        tail = p[:, 8 * VDIM :].astype(f32)
        levels.append(tail[:, 0:8] + tail[:, 8:16] + tail[:, 16:24])
    top = functools.reduce(jnp.maximum, levels)
    weights = [jnp.exp(v - top) for v in levels]
    total = functools.reduce(jnp.add, weights)
    weights = [w / total for w in weights]
    for h in range(8):
        cut = slice(h * VDIM, (h + 1) * VDIM)
        value = sum(p[:, cut].astype(f32) * w[:, h : h + 1] for p, w in zip(parts, weights))
        out_ref[:, cut] = value.astype(bf16)


def project_kernel(info, x0, x1, x2, x3, w_out, out_ref, scr):
    x = info[2]
    rows = jnp.concatenate([x0[...], x1[...], x2[...], x3[...]], axis=0)
    product = nn(rows, w_out[...])
    for d in range(SIDE):
        place = lax.rem(x - d + SIDE, SIDE)
        for y in range(SIDE):
            at = (d * SIDE + y) * 8
            scr[y, place] = product[at : at + 8]
    out_ref[...] = scr[...].reshape(out_ref.shape).astype(bf16)


def dispatch_kernel(info, rows_ref, gain_ref, out_ref, place_ref, gate_ref, scr):
    expert = info[3].astype(f32)
    count, block = rows_ref.shape[0], 16
    features = gain_ref.shape[1]
    hidden = rows_ref[:, :features].astype(f32)
    extra = rows_ref[:, features:].astype(f32)
    hit = extra[:, 0:8] == expert
    mask = jnp.sum(jnp.where(hit, 1.0, 0.0), axis=1, keepdims=True)
    gates = extra[:, 8:16] + extra[:, 16:24] + extra[:, 24:32]
    gate_ref[...] = jnp.sum(jnp.where(hit, gates, 0.0), axis=1, keepdims=True)
    j = lax.broadcasted_iota(jnp.int32, (count, count), 0)
    k = lax.broadcasted_iota(jnp.int32, (count, count), 1)
    before = jnp.where((k < j) & (k // block == j // block), 1.0, 0.0).astype(bf16)
    slot = nn(before, jnp.broadcast_to(mask, (count, 128)).astype(bf16))[:, 0:1]
    j = lax.broadcasted_iota(jnp.int32, (count, out_ref.shape[0]), 0)
    i = lax.broadcasted_iota(jnp.int32, (count, out_ref.shape[0]), 1)
    target = slot.astype(jnp.int32) + CAP * (j // block)
    place = jnp.where((mask > 0.5) & (target == i), 1.0, 0.0).astype(bf16)
    place_ref[...] = place
    scr[:, :features] = (hidden * gain_ref[...]).astype(bf16)
    squares = jnp.sum(hidden * hidden, axis=1, keepdims=True)
    lane = lax.broadcasted_iota(jnp.int32, extra.shape, 1)
    tail = jnp.zeros(extra.shape, f32)
    for part, v in enumerate(split3(squares)):
        tail = jnp.where(lane == part, v, tail)
    scr[:, features:] = tail.astype(bf16)
    out_ref[...] = tn(place, scr[...]).astype(bf16)


def expert_kernel(info, x_ref, w_ref, act_ref):
    shards, rows, _ = x_ref.shape
    features = w_ref.shape[2]
    gate = jnp.zeros((rows, 128), f32)
    upper = jnp.zeros((rows, 128), f32)
    squares = jnp.zeros((rows, 1), f32)
    for s in range(shards):
        x = x_ref[s, :, :features]
        gate += nn(x, w_ref[0, s])
        upper += nn(x, w_ref[1, s])
        tail = x_ref[s, :, features:].astype(f32)
        squares += tail[:, 0:1] + tail[:, 1:2] + tail[:, 2:3]
    factor = lax.rsqrt(squares * (1.0 / (shards * features)) + epsilon)
    gate = gate * factor
    act_ref[...] = (gate * (1.0 / (1.0 + jnp.exp(-gate))) * (upper * factor)).astype(bf16)


def down_kernel(info, act_ref, w_ref, place_ref, gate_ref, near_ref, far_ref):
    shards, rows, _ = act_ref.shape
    total = jnp.zeros((rows, w_ref.shape[2]), f32)
    for s in range(shards):
        total += nn(act_ref[s], w_ref[s])
    high = total.astype(bf16)
    low = (total - high.astype(f32)).astype(bf16)
    place = place_ref[...]
    share = (nn(place, high) + nn(place, low)) * gate_ref[...]
    share = share.reshape(8, 2, 16, share.shape[1])
    near_ref[...] = share[:, 0].reshape(near_ref.shape)
    far_ref[...] = share[:, 1].reshape(far_ref.shape).astype(bf16)


def prompt_kernel(info, q_ref, keys_ref, out_ref, scores, probs):
    pieces = keys_ref.shape[0]
    tokens = q_ref.shape[0]
    me, prefix_len = info[4], info[5]
    queries = jnp.concatenate([q_ref[:, :576], q_ref[:, 576:1152]], axis=0)
    rows = queries.shape[0]
    lane = lax.broadcasted_iota(jnp.int32, (rows, 128), 1)
    token = lax.rem(lax.broadcasted_iota(jnp.int32, (rows, 128), 0), tokens)

    def score(j, top):
        early = nn(queries, keys_ref[j, 0])
        late = nn(queries, keys_ref[j, 1])
        early = jnp.where(lane < prefix_len - j * 128, early, LOW)
        late = jnp.where(lane - token <= (me - j) * tokens, late, LOW)
        scores[j, :, :128] = early
        scores[j, :, 128:] = late
        return jnp.maximum(top, jnp.maximum(early, late))

    top = lax.fori_loop(0, pieces, score, jnp.full((rows, 128), LOW, f32))
    top = jnp.max(top, axis=1, keepdims=True)

    def weigh(j, carry):
        total, weighted = carry
        p = jnp.exp((scores[j] - top) * score_scale)
        keys = jnp.concatenate([keys_ref[j, 0, :LATENT], keys_ref[j, 1, :LATENT]], axis=1)
        return total + (p[:, :128] + p[:, 128:]), weighted + nt(p.astype(bf16), keys)

    total, weighted = lax.fori_loop(
        0, pieces, weigh, (jnp.zeros((rows, 128), f32), jnp.zeros((rows, LATENT), f32))
    )
    result = (weighted / jnp.sum(total, axis=1, keepdims=True)).astype(bf16)
    out_ref[:, :LATENT] = result[:tokens]
    out_ref[:, LATENT:] = result[tokens:]


def prompt_attention(info, queries, keys):
    tokens, width = queries.shape
    pairs = width // 1152
    return pl.pallas_call(
        prompt_kernel,
        out_shape=jax.ShapeDtypeStruct((tokens, pairs * 2 * LATENT), bf16),
        grid=(pairs,),
        in_specs=[
            SMEM,
            pl.BlockSpec((tokens, 1152), lambda i: (0, i)),
            pl.BlockSpec(keys.shape, lambda i: (0, 0, 0, 0)),
        ],
        out_specs=pl.BlockSpec((tokens, 2 * LATENT), lambda i: (0, i)),
        scratch_shapes=[
            pltpu.VMEM((keys.shape[0], 2 * tokens, 256), f32),
            pltpu.VMEM((8, 128), f32),
        ],
        compiler_params=pltpu.CompilerParams(vmem_limit_bytes=48 << 20),
        cost_estimate=pl.CostEstimate(
            flops=2 * 8 * tokens * 4096 * 1088, bytes_accessed=8 << 20, transcendentals=8 * tokens * 4096
        ),
    )(info, queries, keys)


def on_device(
    q_pre,
    prefix_cache,
    span_cache,
    prefix_len,
    q_dec,
    dec_cache,
    cache_len,
    requests,
    w_uv,
    w_out,
    x_dec,
    norm_gain,
    expert_ids,
    expert_gates,
    w_in,
    w_down,
):
    group = lax.axis_index("group")
    seq = lax.axis_index("seq")
    z = lax.axis_index("expert")
    shards = lax.axis_size("seq")
    depth = lax.axis_size("expert")
    info = jnp.stack(
        [group, seq // SIDE, seq % SIDE, group * depth + z, seq, prefix_len[0], z, z]
    ).astype(jnp.int32)
    features = x_dec.shape[1]

    keys = lax.all_gather(jnp.concatenate([prefix_cache, span_cache], axis=0), "seq", axis=0)

    span = span_cache[0]
    q64 = jnp.transpose(q_dec.reshape(8, 8, 576), (1, 0, 2)).reshape(64, 576)
    wanted = jnp.tile(requests.astype(bf16), 8)[:, None]
    packet = jnp.concatenate([q64, jnp.broadcast_to(wanted, (64, 64))], axis=1)
    packets = along_y(packet)
    pieces = along_x(span)
    far = other_core(jnp.stack(pieces))
    rm, rl, rw = call(
        resident_kernel,
        [
            jax.ShapeDtypeStruct((64, 1), f32),
            jax.ShapeDtypeStruct((64, 1), f32),
            jax.ShapeDtypeStruct((64, LATENT), f32),
        ],
        [cache_len, packet, dec_cache],
    )
    part = call(
        span_kernel,
        jax.ShapeDtypeStruct((32, 9 * VDIM), bf16),
        [info, *packets, *pieces, far, w_uv, rm, rl, rw],
        [pltpu.VMEM((SIDE, 8, 9 * VDIM), f32)],
    )
    dec_val = call(
        merge_kernel, jax.ShapeDtypeStruct((32, 8 * VDIM), bf16), [info, *along_y(part)]
    )
    product = call(
        project_kernel,
        jax.ShapeDtypeStruct((128, features), bf16),
        [info, *along_x(dec_val), w_out],
        [pltpu.VMEM((SIDE, SIDE, 8, features), f32)],
    )
    terms = lax.all_to_all(product.reshape(depth, 16, features), "expert", 0, 0, tiled=True)
    hidden = (x_dec.astype(f32) + jnp.sum(terms.astype(f32), axis=0)).astype(bf16)

    g_high = lax.reduce_precision(expert_gates, 8, 7)
    g_mid = lax.reduce_precision(expert_gates - g_high, 8, 7)
    g_low = lax.reduce_precision(expert_gates - g_high - g_mid, 8, 7)
    packed = jnp.concatenate(
        [hidden]
        + [v.astype(bf16) for v in (expert_ids, g_high, g_mid, g_low)]
        + [jnp.zeros((16, 32), bf16)],
        axis=1,
    )
    both = jnp.stack([packed, other_core(packed)])
    rows = everyone(both, "expert", depth).reshape(256, features + 64)
    gain = lax.dynamic_slice(norm_gain, (seq * features,), (features,))[None]
    chosen, place, gate = call(
        dispatch_kernel,
        [
            jax.ShapeDtypeStruct((16 * CAP, features + 64), bf16),
            jax.ShapeDtypeStruct((256, 16 * CAP), bf16),
            jax.ShapeDtypeStruct((256, 1), f32),
        ],
        [info, rows, gain],
        [pltpu.VMEM((256, features + 64), bf16)],
    )
    arrived = everyone(chosen, "seq", shards)
    act = call(
        expert_kernel,
        jax.ShapeDtypeStruct((16 * CAP, 128), bf16),
        [info, arrived, w_in[0].reshape(2, shards, features, 128)],
    )
    w_back = lax.all_to_all(
        jnp.transpose(w_down[0].reshape(128, shards, features), (1, 0, 2)), "seq", 0, 0, tiled=True
    )
    acts = everyone(act, "seq", shards)
    near, far_share = call(
        down_kernel,
        [
            jax.ShapeDtypeStruct((128, features), f32),
            jax.ShapeDtypeStruct((128, features), bf16),
        ],
        [info, acts, w_back, place, gate],
    )
    share = (near + other_core(far_share).astype(f32)).astype(bf16)
    shares = lax.all_to_all(share.reshape(depth, 16, features), "expert", 0, 0, tiled=True)
    h_out = (hidden.astype(f32) + jnp.sum(shares.astype(f32), axis=0)).astype(bf16)

    o_pre = prompt_attention(info, q_pre[0], keys)[None]
    return (o_pre, h_out)


def solution(mesh):
    return jax.shard_map(
        on_device,
        mesh=mesh,
        in_specs=(
            P("group", "seq", "expert"),
            P("group", None, "seq"),
            P("group", None, "seq"),
            P("group"),
            P(("group", "seq"), "expert"),
            P(("group", "seq"), None, None),
            P(("group", "seq")),
            P(("group", "seq")),
            P("expert", None, None),
            P("expert", "seq"),
            P(("group", "expert"), "seq"),
            P(),
            P(("group", "expert"), None),
            P(("group", "expert"), None),
            P(("group", "expert"), None, None, "seq"),
            P(("group", "expert"), "seq", None),
        ),
        out_specs=(P("group", "seq", "expert"), P(("group", "expert"), "seq")),
        check_vma=False,
    )
```

```python
import functools

import jax
import jax.numpy as jnp
from jax import lax
from jax.experimental import pallas as pl
from jax.experimental.pallas import tpu as pltpu
from jax.sharding import PartitionSpec as P

LATENT = 512
VDIM = 128
SIDE = 4
CAP = 12

ROWS_X = [[y * SIDE + x for x in range(SIDE)] for y in range(SIDE)]
ROWS_Y = [[y * SIDE + x for y in range(SIDE)] for x in range(SIDE)]

bf16 = jnp.bfloat16
f32 = jnp.float32
score_scale = 192.0 ** (-0.5)
epsilon = 1e-06
LOW = -1e30

VMEM = pl.BlockSpec(memory_space=pltpu.VMEM)
SMEM = pl.BlockSpec(memory_space=pltpu.SMEM)


def call(kernel, out_shape, ins, scratch=(), fetch=(), cost=None, limit=48 << 20):
    multi = isinstance(out_shape, (tuple, list))

    def body(*refs):
        refs = list(refs)
        if fetch:
            held, sems = refs[-len(fetch) - 1 : -1], refs[-1]
            copies = [
                pltpu.make_async_copy(refs[at], to, sems.at[i])
                for i, (at, to) in enumerate(zip(fetch, held))
            ]
            for copy in copies:
                copy.start()
            for copy in copies:
                copy.wait()
            refs = refs[: -len(fetch) - 1]
            for at, to in zip(fetch, held):
                refs[at] = to
        kernel(*refs)

    held = [pltpu.VMEM(ins[at].shape, ins[at].dtype) for at in fetch]
    if fetch:
        held.append(pltpu.SemaphoreType.DMA((len(fetch),)))
    place = [SMEM] + [VMEM] * (len(ins) - 1)
    for at in fetch:
        place[at] = pl.BlockSpec(memory_space=pl.ANY)
    return pl.pallas_call(
        body,
        out_shape=out_shape,
        in_specs=place,
        out_specs=[VMEM] * len(out_shape) if multi else VMEM,
        scratch_shapes=list(scratch) + held,
        compiler_params=pltpu.CompilerParams(vmem_limit_bytes=limit),
        cost_estimate=cost,
    )(*ins)


def nn(a, b):
    return jnp.dot(a, b, preferred_element_type=f32)


def nt(a, b):
    return lax.dot_general(a, b, (((1,), (1,)), ((), ())), preferred_element_type=f32)


def tn(a, b):
    return lax.dot_general(a, b, (((0,), (0,)), ((), ())), preferred_element_type=f32)


def split3(v):
    high = v.astype(bf16).astype(f32)
    rest = v - high
    mid = rest.astype(bf16).astype(f32)
    return high, mid, (rest - mid).astype(bf16).astype(f32)


def to_x(array, d):
    return lax.ppermute(
        array,
        "seq",
        [(y * SIDE + x, y * SIDE + (x + d) % SIDE) for y in range(SIDE) for x in range(SIDE)],
    )


def to_y(array, d):
    return lax.ppermute(
        array,
        "seq",
        [(y * SIDE + x, (y + d) % SIDE * SIDE + x) for y in range(SIDE) for x in range(SIDE)],
    )


def along_x(array):
    return [array] + [to_x(array, d) for d in range(1, SIDE)]


def along_y(array):
    return [array] + [to_y(array, d) for d in range(1, SIDE)]


def other_core(array):
    return lax.ppermute(array, "group", [(0, 1), (1, 0)])


def everyone(array, axis, count, groups=None):
    return lax.all_to_all(
        jnp.broadcast_to(array[None], (count,) + array.shape),
        axis,
        0,
        0,
        tiled=True,
        axis_index_groups=groups,
    )


def head_rows(ref):
    raw = ref[...].astype(f32)
    heads = [raw[:, h * 576 : (h + 1) * 576] for h in range(8)]
    wanted = raw[:, 8 * 576 : 8 * 576 + 1]
    return jnp.concatenate(heads, axis=0).astype(bf16), jnp.concatenate([wanted] * 8, axis=0)


def resident_kernel(lens, q_ref, cache_ref, m_ref, l_ref, w_ref):
    count = cache_ref.shape[0]
    queries, _ = head_rows(q_ref)
    row = lax.rem(lax.broadcasted_iota(jnp.int32, (queries.shape[0], 128), 0), count)
    column = lax.broadcasted_iota(jnp.int32, (queries.shape[0], 128), 1)
    scores = []
    for r in range(count):
        s = nn(queries, cache_ref[r]) * score_scale
        scores.append(jnp.where((row == r) & (column < lens[r]), s, LOW))
    top = scores[0]
    for s in scores[1:]:
        top = jnp.maximum(top, s)
    m = jnp.max(top, axis=1, keepdims=True)
    total = jnp.zeros_like(top)
    weighted = jnp.zeros((queries.shape[0], LATENT), f32)
    for r in range(count):
        p = jnp.where((row == r) & (column < lens[r]), jnp.exp(scores[r] - m), 0.0)
        total += p
        weighted += nt(p.astype(bf16), cache_ref[r, :LATENT])
    m_ref[...] = m
    l_ref[...] = jnp.sum(total, axis=1, keepdims=True)
    w_ref[...] = weighted


def span_kernel(
    info, q0, q1, q2, q3, k0, k1, k2, k3, kp, w_uv, rm, rl, rw, out_ref, scr
):
    group = info[0].astype(f32)
    y = info[1]
    parts = [head_rows(q) for q in (q0, q1, q2, q3)]
    queries = jnp.concatenate([p[0] for p in parts], axis=0)
    wanted = jnp.concatenate([p[1] for p in parts], axis=0)
    own_keys = jnp.concatenate([k0[...], k1[...], k2[...], k3[...]], axis=1)
    far_keys = jnp.concatenate([kp[0], kp[1], kp[2], kp[3]], axis=1)
    own = wanted == group
    valid = wanted < 1.5
    s = jnp.where(own, nn(queries, own_keys), nn(queries, far_keys)) * score_scale
    m = jnp.where(valid, jnp.max(s, axis=1, keepdims=True), LOW)
    p = jnp.where(valid, jnp.exp(s - m), 0.0)
    total = jnp.sum(p, axis=1, keepdims=True)
    weighted = nt(jnp.where(own, p, 0.0).astype(bf16), own_keys[:LATENT]) + nt(
        jnp.where(own, 0.0, p).astype(bf16), far_keys[:LATENT]
    )
    here = rm.shape[0]
    newest = jnp.maximum(m[:here], rm[...])
    a = jnp.exp(m[:here] - newest)
    b = jnp.exp(rm[...] - newest)
    m = jnp.concatenate([newest, m[here:]], axis=0)
    total = jnp.concatenate([total[:here] * a + rl[...] * b, total[here:]], axis=0)
    weighted = jnp.concatenate([weighted[:here] * a + rw[...] * b, weighted[here:]], axis=0)
    some = total > 0.0
    safe = jnp.where(some, total, 1.0)
    latent = (weighted / safe).reshape(SIDE, 8, 8, LATENT)
    level = jnp.where(some, m + jnp.log(safe), LOW).reshape(SIDE, 8, 8, 1)
    lane = lax.broadcasted_iota(jnp.int32, (SIDE, 8, 128), 2)
    tail = jnp.zeros((SIDE, 8, 128), f32)
    places = [lax.rem(y - d + SIDE, SIDE) for d in range(SIDE)]
    for h in range(8):
        rows = latent[:, h].reshape(SIDE * 8, LATENT).astype(bf16)
        value = nn(rows, w_uv[h])
        for d in range(SIDE):
            scr[places[d], :, h * VDIM : (h + 1) * VDIM] = value[d * 8 : (d + 1) * 8]
        for part, v in enumerate(split3(level[:, h])):
            tail = jnp.where(lane == part * 8 + h, v, tail)
    for d in range(SIDE):
        scr[places[d], :, 8 * VDIM :] = tail[d]
    out_ref[...] = scr[...].reshape(SIDE * 8, 9 * VDIM).astype(bf16)


def merge_kernel(info, p0, p1, p2, p3, out_ref):
    parts = [p0, p1, p2, p3]
    levels = []
    for p in parts:
        tail = p[:, 8 * VDIM :].astype(f32)
        levels.append(tail[:, 0:8] + tail[:, 8:16] + tail[:, 16:24])
    top = functools.reduce(jnp.maximum, levels)
    weights = [jnp.exp(v - top) for v in levels]
    total = functools.reduce(jnp.add, weights)
    weights = [w / total for w in weights]
    for h in range(8):
        cut = slice(h * VDIM, (h + 1) * VDIM)
        value = sum(p[:, cut].astype(f32) * w[:, h : h + 1] for p, w in zip(parts, weights))
        out_ref[:, cut] = value.astype(bf16)


def project_kernel(info, x0, x1, x2, x3, w_out, out_ref, scr):
    x = info[2]
    rows = jnp.concatenate([x0[...], x1[...], x2[...], x3[...]], axis=0)
    product = nt(rows, w_out[...])
    for d in range(SIDE):
        place = lax.rem(x - d + SIDE, SIDE)
        for y in range(SIDE):
            at = (d * SIDE + y) * 8
            scr[y, place] = product[at : at + 8]
    out_ref[...] = scr[...].reshape(out_ref.shape).astype(bf16)


def hidden_kernel(info, terms_ref, x_ref, gain_ref, extra_ref, hidden_ref, packed_ref):
    attention = jnp.sum(terms_ref[...].astype(f32), axis=0)
    rounded = (x_ref[...].astype(f32) + attention).astype(bf16)
    hidden_ref[...] = rounded
    hidden = rounded.astype(f32)
    features = hidden.shape[1]
    packed_ref[:, :features] = (hidden * gain_ref[...]).astype(bf16)
    extra = extra_ref[...]
    lane = lax.broadcasted_iota(jnp.int32, extra.shape, 1)
    for part, v in enumerate(split3(jnp.sum(hidden * hidden, axis=1, keepdims=True))):
        extra = jnp.where(lane == 32 + part, v, extra)
    packed_ref[:, features:] = extra.astype(bf16)


def expert_kernel(info, near_ref, far_ref, w_ref, act_ref, place_ref, gate_ref):
    shards, half, _ = near_ref.shape
    features, block = w_ref.shape[2], 16
    rows, slots = 2 * half, act_ref.shape[0]
    both = jnp.zeros((rows, 256), f32)
    tails = jnp.zeros((rows, 64), f32)
    for s in range(shards):
        x = jnp.concatenate([near_ref[s], far_ref[s]], axis=0)
        both += nn(x[:, :features], jnp.concatenate([w_ref[0, s], w_ref[1, s]], axis=1))
        tails += x[:, features:].astype(f32)
    squares = tails[:, 32:33] + tails[:, 33:34] + tails[:, 34:35]
    factor = lax.rsqrt(squares * (1.0 / (shards * features)) + epsilon)
    gate = both[:, :128] * factor
    act = (gate * (1.0 / (1.0 + jnp.exp(-gate))) * (both[:, 128:] * factor)).astype(bf16)
    extra = jnp.concatenate([near_ref[0, :, features:], far_ref[0, :, features:]], axis=0).astype(f32)
    hit = extra[:, 0:8] == info[3].astype(f32)
    mask = jnp.sum(jnp.where(hit, 1.0, 0.0), axis=1, keepdims=True)
    gates = extra[:, 8:16] + extra[:, 16:24] + extra[:, 24:32]
    gate_ref[...] = jnp.sum(jnp.where(hit, gates, 0.0), axis=1, keepdims=True)
    j = lax.broadcasted_iota(jnp.int32, (rows, rows), 0)
    k = lax.broadcasted_iota(jnp.int32, (rows, rows), 1)
    before = jnp.where((k < j) & (k // block == j // block), 1.0, 0.0).astype(bf16)
    slot = nn(before, jnp.broadcast_to(mask, (rows, 128)).astype(bf16))[:, 0:1]
    j = lax.broadcasted_iota(jnp.int32, (rows, slots), 0)
    i = lax.broadcasted_iota(jnp.int32, (rows, slots), 1)
    target = slot.astype(jnp.int32) + CAP * (j // block)
    place = jnp.where((mask > 0.5) & (target == i), 1.0, 0.0).astype(bf16)
    place_ref[...] = place
    act_ref[...] = tn(place, act).astype(bf16)


def down_kernel(info, a0, a1, a2, a3, w0, w1, w2, w3, place_ref, gate_ref, near_ref, far_ref):
    y = info[1]
    place, gates = place_ref[...], gate_ref[...]
    half = near_ref.shape[1]
    for d in range(SIDE):
        to = lax.rem(y + d, SIDE)
        total = sum(nt(a[...], w[to]) for a, w in ((a0, w0), (a1, w1), (a2, w2), (a3, w3)))
        high = total.astype(bf16)
        low = (total - high.astype(f32)).astype(bf16)
        share = (nn(place, high) + nn(place, low)) * gates
        near_ref[d] = share[:half]
        far_ref[d] = share[half:].astype(bf16)


def prompt_kernel(info, q_ref, keys_ref, out_ref, scores, weighted):
    pieces, tokens = keys_ref.shape[0], q_ref.shape[0]
    heads = q_ref.shape[1] // 576
    me, prefix_len = info[4], info[5]
    queries = jnp.concatenate([q_ref[:, h * 576 : (h + 1) * 576] for h in range(heads)], axis=0)
    rows = queries.shape[0]
    lane = lax.broadcasted_iota(jnp.int32, (tokens, 128), 1)
    ahead = lane - lax.broadcasted_iota(jnp.int32, (tokens, 128), 0)
    unroll = 8

    def score(i, top):
        for u in range(unroll):
            j = i * unroll + u
            early = jnp.where(lane < prefix_len - j * 128, 0.0, LOW)
            late = jnp.where(ahead <= (me - j) * tokens, 0.0, LOW)
            masks = jnp.concatenate([jnp.concatenate([early, late], axis=1)] * heads, axis=0)
            s = nn(queries, keys_ref[j]) + masks
            scores[j] = s
            top = jnp.maximum(top, jnp.maximum(s[:, :128], s[:, 128:]))
        return top

    top = lax.fori_loop(0, pieces // unroll, score, jnp.full((rows, 128), LOW, f32))
    top = jnp.max(top, axis=1, keepdims=True) * score_scale
    weighted[...] = jnp.zeros_like(weighted)

    def weigh(i, total):
        sums = jnp.zeros(weighted.shape, f32)
        for u in range(unroll):
            j = i * unroll + u
            p = jnp.exp(scores[j] * score_scale - top)
            total = total + (p[:, :128] + p[:, 128:])
            sums = sums + nt(p.astype(bf16), keys_ref[j, :LATENT])
        weighted[...] += sums
        return total

    total = lax.fori_loop(0, pieces // unroll, weigh, jnp.zeros((rows, 128), f32))
    total = jnp.sum(total, axis=1, keepdims=True)
    result = (weighted[...] / total).astype(bf16)
    for h in range(heads):
        out_ref[:, h * LATENT : (h + 1) * LATENT] = result[h * tokens : (h + 1) * tokens]


def prompt_attention(info, queries, keys, heads=4):
    tokens, width = queries.shape
    steps = width // (576 * heads)
    pieces = keys.shape[0]
    return pl.pallas_call(
        prompt_kernel,
        out_shape=jax.ShapeDtypeStruct((tokens, steps * heads * LATENT), bf16),
        grid=(steps,),
        in_specs=[
            SMEM,
            pl.BlockSpec((tokens, heads * 576), lambda i: (0, i)),
            pl.BlockSpec(keys.shape, lambda i: (0, 0, 0)),
        ],
        out_specs=pl.BlockSpec((tokens, heads * LATENT), lambda i: (0, i)),
        scratch_shapes=[
            pltpu.VMEM((pieces, heads * tokens, 256), f32),
            pltpu.VMEM((heads * tokens, LATENT), f32),
        ],
        compiler_params=pltpu.CompilerParams(vmem_limit_bytes=48 << 20),
        cost_estimate=pl.CostEstimate(
            flops=2 * 8 * tokens * 4096 * 1088, bytes_accessed=8 << 20, transcendentals=8 * tokens * 4096
        ),
    )(info, queries, keys)


def on_device(
    q_pre,
    prefix_cache,
    span_cache,
    prefix_len,
    q_dec,
    dec_cache,
    cache_len,
    requests,
    w_uv,
    w_out,
    x_dec,
    norm_gain,
    expert_ids,
    expert_gates,
    w_in,
    w_down,
):
    group = lax.axis_index("group")
    seq = lax.axis_index("seq")
    z = lax.axis_index("expert")
    shards = lax.axis_size("seq")
    depth = lax.axis_size("expert")
    info = jnp.stack(
        [group, seq // SIDE, seq % SIDE, group * depth + z, seq, prefix_len[0], z, z]
    ).astype(jnp.int32)
    features = x_dec.shape[1]

    wanted = jnp.broadcast_to(requests.astype(bf16)[:, None], (8, 128))
    packet = jnp.concatenate([q_dec, wanted], axis=1)
    span, packet, prefix, columns = lax.optimization_barrier(
        (span_cache[0], packet, prefix_cache[0], span_cache[0])
    )
    keys = lax.all_gather(jnp.concatenate([prefix, columns], axis=1), "seq", axis=0)
    pieces, packets = along_x(span), along_y(packet)
    resident = call(
        resident_kernel,
        [
            jax.ShapeDtypeStruct((64, 1), f32),
            jax.ShapeDtypeStruct((64, 1), f32),
            jax.ShapeDtypeStruct((64, LATENT), f32),
        ],
        [cache_len, packet, dec_cache],
    )
    w_back = w_down[0].T.reshape(SIDE, SIDE, features, 128).transpose(1, 0, 2, 3)
    pieces, packets, resident, w_back = lax.optimization_barrier(
        (pieces, packets, resident, w_back)
    )
    far = other_core(jnp.stack(pieces))
    part = call(
        span_kernel,
        jax.ShapeDtypeStruct((32, 9 * VDIM), bf16),
        [info, *packets, *pieces, far, w_uv, *resident],
        [pltpu.VMEM((SIDE, 8, 9 * VDIM), f32)],
        fetch=(5, 6, 7, 8, 9),
    )

    dec_val = call(
        merge_kernel,
        jax.ShapeDtypeStruct((32, 8 * VDIM), bf16),
        [info, *along_y(part)],
        fetch=(1, 2, 3, 4),
    )
    product = call(
        project_kernel,
        jax.ShapeDtypeStruct((128, features), bf16),
        [info, *along_x(dec_val), w_out.T],
        [pltpu.VMEM((SIDE, SIDE, 8, features), f32)],
        fetch=(1, 2, 3, 4),
    )
    product, w_back = lax.optimization_barrier((product, w_back))
    x_here = seq % SIDE
    w_back = [
        lax.dynamic_index_in_dim(w_back, (x_here + d) % SIDE, 0, keepdims=False)
        for d in range(SIDE)
    ]
    w_back = [w_back[0]] + [to_x(w_back[d], d) for d in range(1, SIDE)]
    terms = lax.all_to_all(product.reshape(depth, 16, features), "expert", 0, 0, tiled=True)

    g_high = lax.reduce_precision(expert_gates, 8, 7)
    g_mid = lax.reduce_precision(expert_gates - g_high, 8, 7)
    g_low = lax.reduce_precision(expert_gates - g_high - g_mid, 8, 7)
    extra = jnp.concatenate(
        [expert_ids.astype(f32), g_high, g_mid, g_low, jnp.zeros((16, 32), f32)], axis=1
    )
    gain = lax.dynamic_slice(norm_gain, (seq * features,), (features,))[None]
    hidden, packed = call(
        hidden_kernel,
        [
            jax.ShapeDtypeStruct((16, features), bf16),
            jax.ShapeDtypeStruct((16, features + 64), bf16),
        ],
        [info, terms, x_dec, gain, extra],
    )
    rows = everyone(packed, "expert", depth).reshape(16 * depth, features + 64)
    rows, q_pre, keys, w_back = lax.optimization_barrier((rows, q_pre, keys, w_back))
    arrived = everyone(rows, "seq", shards)
    o_pre = prompt_attention(info, q_pre[0], keys)[None]
    arrived, o_pre = lax.optimization_barrier((arrived, o_pre))
    act, place, gate = call(
        expert_kernel,
        [
            jax.ShapeDtypeStruct((16 * CAP, 128), bf16),
            jax.ShapeDtypeStruct((256, 16 * CAP), bf16),
            jax.ShapeDtypeStruct((256, 1), f32),
        ],
        [info, arrived, other_core(arrived), w_in[0].reshape(2, shards, features, 128)],
    )
    shape = (SIDE, 16 * depth, features)
    near, far_share = call(
        down_kernel,
        [jax.ShapeDtypeStruct(shape, f32), jax.ShapeDtypeStruct(shape, bf16)],
        [info, *along_x(act), *w_back, place, gate],
    )
    share = (near + other_core(far_share).astype(f32)).astype(bf16)
    parts = [share[0]] + [to_y(share[d], d) for d in range(1, SIDE)]
    share = sum(v.astype(f32) for v in parts).astype(bf16)
    shares = lax.all_to_all(share.reshape(depth, 16, features), "expert", 0, 0, tiled=True)
    h_out = (hidden.astype(f32) + jnp.sum(shares.astype(f32), axis=0)).astype(bf16)

    return (o_pre, h_out)


def solution(mesh):
    return jax.shard_map(
        on_device,
        mesh=mesh,
        in_specs=(
            P("group", "seq", "expert"),
            P("group", None, "seq"),
            P("group", None, "seq"),
            P("group"),
            P(("group", "seq"), "expert"),
            P(("group", "seq"), None, None),
            P(("group", "seq")),
            P(("group", "seq")),
            P("expert", None, None),
            P("expert", "seq"),
            P(("group", "expert"), "seq"),
            P(),
            P(("group", "expert"), None),
            P(("group", "expert"), None),
            P(("group", "expert"), None, None, "seq"),
            P(("group", "expert"), "seq", None),
        ),
        out_specs=(P("group", "seq", "expert"), P(("group", "expert"), "seq")),
        check_vma=False,
    )
```

```python
import functools

import jax
import jax.numpy as jnp
from jax import lax
from jax.experimental import pallas as pl
from jax.experimental.pallas import tpu as pltpu
from jax.sharding import PartitionSpec as P

LATENT = 512
VDIM = 128
SIDE = 4
CAP = 12

ROWS_X = [[y * SIDE + x for x in range(SIDE)] for y in range(SIDE)]
ROWS_Y = [[y * SIDE + x for y in range(SIDE)] for x in range(SIDE)]

bf16 = jnp.bfloat16
f32 = jnp.float32
score_scale = 192.0 ** (-0.5)
epsilon = 1e-06
LOW = -1e30

VMEM = pl.BlockSpec(memory_space=pltpu.VMEM)
SMEM = pl.BlockSpec(memory_space=pltpu.SMEM)


def call(kernel, out_shape, ins, scratch=(), fetch=(), mib=8):
    multi = isinstance(out_shape, (tuple, list))

    def body(*refs):
        refs = list(refs)
        if fetch:
            held, sems = refs[-len(fetch) - 1 : -1], refs[-1]
            copies = [
                pltpu.make_async_copy(refs[at], to, sems.at[i])
                for i, (at, to) in enumerate(zip(fetch, held))
            ]
            for copy in copies:
                copy.start()
            for copy in copies:
                copy.wait()
            refs = refs[: -len(fetch) - 1]
            for at, to in zip(fetch, held):
                refs[at] = to
        kernel(*refs)

    held = [pltpu.VMEM(ins[at].shape, ins[at].dtype) for at in fetch]
    if fetch:
        held.append(pltpu.SemaphoreType.DMA((len(fetch),)))
    place = [SMEM] + [VMEM] * (len(ins) - 1)
    for at in fetch:
        place[at] = pl.BlockSpec(memory_space=pltpu.HBM)
    return pl.pallas_call(
        body,
        out_shape=out_shape,
        in_specs=place,
        out_specs=[VMEM] * len(out_shape) if multi else VMEM,
        scratch_shapes=list(scratch) + held,
        compiler_params=pltpu.CompilerParams(vmem_limit_bytes=mib << 20),
    )(*[in_hbm(v) if i in fetch else v for i, v in enumerate(ins)])


def in_hbm(array):
    return pltpu.with_memory_space_constraint(array, pltpu.HBM)


def nn(a, b):
    return jnp.dot(a, b, preferred_element_type=f32)


def nt(a, b):
    return lax.dot_general(a, b, (((1,), (1,)), ((), ())), preferred_element_type=f32)


def tn(a, b):
    return lax.dot_general(a, b, (((0,), (0,)), ((), ())), preferred_element_type=f32)


def split3(v):
    high = v.astype(bf16).astype(f32)
    rest = v - high
    mid = rest.astype(bf16).astype(f32)
    return high, mid, (rest - mid).astype(bf16).astype(f32)


def to_x(array, d):
    return lax.ppermute(
        array,
        "seq",
        [(y * SIDE + x, y * SIDE + (x + d) % SIDE) for y in range(SIDE) for x in range(SIDE)],
    )


def to_y(array, d):
    return lax.ppermute(
        array,
        "seq",
        [(y * SIDE + x, (y + d) % SIDE * SIDE + x) for y in range(SIDE) for x in range(SIDE)],
    )


NEIGHBOURS = (0, 1, SIDE, SIDE + 1)
SQUARES = (0, 2, 2 * SIDE, 2 * SIDE + 2)


def swap(array, mask):
    return lax.ppermute(array, "seq", [(i, i ^ mask) for i in range(SIDE * SIDE)])


def along_x(array):
    return [array] + [to_x(array, d) for d in range(1, SIDE)]


def along_y(array):
    return [array] + [to_y(array, d) for d in range(1, SIDE)]


def other_core(array):
    return lax.ppermute(array, "group", [(0, 1), (1, 0)])


def everyone(array, axis, count, groups=None):
    return lax.all_to_all(
        jnp.broadcast_to(array[None], (count,) + array.shape),
        axis,
        0,
        0,
        tiled=True,
        axis_index_groups=groups,
    )


def head_rows(ref):
    raw = ref[...].astype(f32)
    heads = [raw[h // 4 * 8 : h // 4 * 8 + 8, h % 4 * 576 : h % 4 * 576 + 576] for h in range(8)]
    wanted = raw[:8, 4 * 576 : 4 * 576 + 1]
    return jnp.concatenate(heads, axis=0).astype(bf16), jnp.concatenate([wanted] * 8, axis=0)


def resident_kernel(lens, q_ref, cache_hbm, k0, k1, k2, k3, state_ref, stack, cache_ref, held, sem, ins, out_sem):
    cache_copy = pltpu.make_async_copy(cache_hbm, cache_ref, sem)
    cache_copy.start()
    copies = [
        pltpu.make_async_copy(k, held.at[d], ins.at[d]) for d, k in enumerate((k0, k1, k2, k3))
    ]
    for copy in copies:
        copy.start()
    queries, _ = head_rows(q_ref)
    for copy in copies:
        copy.wait()
    out = pltpu.make_async_copy(held, stack, out_sem)
    out.start()
    cache_copy.wait()
    count = cache_ref.shape[0]
    row = lax.rem(lax.broadcasted_iota(jnp.int32, (queries.shape[0], 128), 0), count)
    column = lax.broadcasted_iota(jnp.int32, (queries.shape[0], 128), 1)
    scores = []
    for r in range(count):
        s = nn(queries, cache_ref[r]) * score_scale
        scores.append(jnp.where((row == r) & (column < lens[r]), s, LOW))
    top = scores[0]
    for s in scores[1:]:
        top = jnp.maximum(top, s)
    m = jnp.max(top, axis=1, keepdims=True)
    total = jnp.zeros_like(top)
    weighted = jnp.zeros((queries.shape[0], LATENT), f32)
    for r in range(count):
        p = jnp.where((row == r) & (column < lens[r]), jnp.exp(scores[r] - m), 0.0)
        total += p
        weighted += nt(p.astype(bf16), cache_ref[r, :LATENT])
    state_ref[:, :LATENT] = weighted
    state_ref[:, LATENT : LATENT + 128] = jnp.broadcast_to(m, total.shape)
    state_ref[:, LATENT + 128 :] = jnp.broadcast_to(jnp.sum(total, axis=1, keepdims=True), total.shape)
    out.wait()


def resident_attention(cache_len, packet, dec_cache, pieces):
    hbm = pl.BlockSpec(memory_space=pltpu.HBM)
    stack = (SIDE,) + pieces[0].shape
    return pl.pallas_call(
        resident_kernel,
        out_shape=[
            jax.ShapeDtypeStruct((64, LATENT + 256), f32),
            jax.ShapeDtypeStruct(stack, bf16),
        ],
        in_specs=[SMEM, VMEM] + [hbm] * 5,
        out_specs=[VMEM, hbm],
        scratch_shapes=[
            pltpu.VMEM(dec_cache.shape, bf16),
            pltpu.VMEM(stack, bf16),
            pltpu.SemaphoreType.DMA,
            pltpu.SemaphoreType.DMA((SIDE,)),
            pltpu.SemaphoreType.DMA,
        ],
        compiler_params=pltpu.CompilerParams(vmem_limit_bytes=8 << 20),
    )(cache_len, packet, in_hbm(dec_cache), *[in_hbm(piece) for piece in pieces])


def span_kernel(
    info, q0, q1, q2, q3, k0, k1, k2, k3, kp, w_uv, state, out_ref, scr
):
    group = info[0].astype(f32)
    y = info[1]
    parts = [head_rows(q) for q in (q0, q1, q2, q3)]
    queries = jnp.concatenate([p[0] for p in parts], axis=0)
    wanted = jnp.concatenate([p[1] for p in parts], axis=0)
    own_keys = jnp.concatenate([k0[...], k1[...], k2[...], k3[...]], axis=1)
    far_keys = jnp.concatenate([kp[0], kp[1], kp[2], kp[3]], axis=1)
    own = wanted == group
    valid = wanted < 1.5
    s = jnp.where(own, nn(queries, own_keys), nn(queries, far_keys)) * score_scale
    m = jnp.where(valid, jnp.max(s, axis=1, keepdims=True), LOW)
    p = jnp.where(valid, jnp.exp(s - m), 0.0)
    total = jnp.sum(p, axis=1, keepdims=True)
    weighted = nt(jnp.where(own, p, 0.0).astype(bf16), own_keys[:LATENT]) + nt(
        jnp.where(own, 0.0, p).astype(bf16), far_keys[:LATENT]
    )
    here = state.shape[0]
    rw = state[:, :LATENT]
    rm = state[:, LATENT : LATENT + 1]
    rl = state[:, LATENT + 128 : LATENT + 129]
    newest = jnp.maximum(m[:here], rm)
    a = jnp.exp(m[:here] - newest)
    b = jnp.exp(rm - newest)
    m = jnp.concatenate([newest, m[here:]], axis=0)
    total = jnp.concatenate([total[:here] * a + rl * b, total[here:]], axis=0)
    weighted = jnp.concatenate([weighted[:here] * a + rw * b, weighted[here:]], axis=0)
    some = total > 0.0
    safe = jnp.where(some, total, 1.0)
    latent = (weighted / safe).reshape(SIDE, 8, 8, LATENT)
    level = jnp.where(some, m + jnp.log(safe), LOW).reshape(SIDE, 8, 8, 1)
    lane = lax.broadcasted_iota(jnp.int32, (SIDE, 8, 128), 2)
    tail = jnp.zeros((SIDE, 8, 128), f32)
    places = [lax.rem(y - d + SIDE, SIDE) for d in range(SIDE)]
    for h in range(8):
        rows = latent[:, h].reshape(SIDE * 8, LATENT).astype(bf16)
        value = nn(rows, w_uv[h])
        for d in range(SIDE):
            scr[places[d], :, h * VDIM : (h + 1) * VDIM] = value[d * 8 : (d + 1) * 8]
        for part, v in enumerate(split3(level[:, h])):
            tail = jnp.where(lane == part * 8 + h, v, tail)
    for d in range(SIDE):
        scr[places[d], :, 8 * VDIM :] = tail[d]
    out_ref[...] = scr[...].reshape(SIDE * 8, 9 * VDIM).astype(bf16)


def merge_kernel(info, p0, p1, p2, p3, out_ref):
    parts = [p0, p1, p2, p3]
    levels = []
    for p in parts:
        tail = p[:, 8 * VDIM :].astype(f32)
        levels.append(tail[:, 0:8] + tail[:, 8:16] + tail[:, 16:24])
    top = functools.reduce(jnp.maximum, levels)
    weights = [jnp.exp(v - top) for v in levels]
    total = functools.reduce(jnp.add, weights)
    weights = [w / total for w in weights]
    for h in range(8):
        cut = slice(h * VDIM, (h + 1) * VDIM)
        value = sum(p[:, cut].astype(f32) * w[:, h : h + 1] for p, w in zip(parts, weights))
        out_ref[:, cut] = value.astype(bf16)


def project_kernel(info, x0, x1, x2, x3, w_out, out_ref, scr):
    x = info[2]
    rows = jnp.concatenate([x0[...], x1[...], x2[...], x3[...]], axis=0)
    product = nt(rows, w_out[...])
    for d in range(SIDE):
        place = lax.rem(x - d + SIDE, SIDE)
        for y in range(SIDE):
            at = (d * SIDE + y) * 8
            scr[y, place] = product[at : at + 8]
    out_ref[...] = scr[...].reshape(out_ref.shape).astype(bf16)


def hidden_kernel(info, terms_ref, x_ref, gain_ref, extra_ref, hidden_ref, packed_ref):
    attention = jnp.sum(terms_ref[...].astype(f32), axis=0)
    rounded = (x_ref[...].astype(f32) + attention).astype(bf16)
    hidden_ref[...] = rounded
    hidden = rounded.astype(f32)
    features = hidden.shape[1]
    packed_ref[:, :features] = (hidden * gain_ref[...]).astype(bf16)
    extra = extra_ref[...]
    lane = lax.broadcasted_iota(jnp.int32, extra.shape, 1)
    for part, v in enumerate(split3(jnp.sum(hidden * hidden, axis=1, keepdims=True))):
        extra = jnp.where(lane == 32 + part, v, extra)
    packed_ref[:, features:] = extra.astype(bf16)


def expert_kernel(info, near_ref, far_ref, w_hbm, act_ref, place_ref, gate_ref, w_ref, sems):
    copies = [
        pltpu.make_async_copy(
            w_hbm.at[:, pl.ds(i * SIDE, SIDE)], w_ref.at[:, pl.ds(i * SIDE, SIDE)], sems.at[i]
        )
        for i in range(SIDE)
    ]
    for copy in copies:
        copy.start()
    shards, half, _ = near_ref.shape
    features, block = w_ref.shape[2], 16
    rows, slots = 2 * half, act_ref.shape[0]
    both = jnp.zeros((rows, 256), f32)
    tails = jnp.zeros((rows, 64), f32)
    for s in range(shards):
        if s % SIDE == 0:
            copies[s // SIDE].wait()
        x = jnp.concatenate([near_ref[s], far_ref[s]], axis=0)
        both += nn(x[:, :features], jnp.concatenate([w_ref[0, s], w_ref[1, s]], axis=1))
        tails += x[:, features:].astype(f32)
    squares = tails[:, 32:33] + tails[:, 33:34] + tails[:, 34:35]
    factor = lax.rsqrt(squares * (1.0 / (shards * features)) + epsilon)
    gate = both[:, :128] * factor
    act = (gate * (1.0 / (1.0 + jnp.exp(-gate))) * (both[:, 128:] * factor)).astype(bf16)
    extra = jnp.concatenate([near_ref[0, :, features:], far_ref[0, :, features:]], axis=0).astype(f32)
    hit = extra[:, 0:8] == info[3].astype(f32)
    mask = jnp.sum(jnp.where(hit, 1.0, 0.0), axis=1, keepdims=True)
    gates = extra[:, 8:16] + extra[:, 16:24] + extra[:, 24:32]
    gate_ref[...] = jnp.sum(jnp.where(hit, gates, 0.0), axis=1, keepdims=True)
    j = lax.broadcasted_iota(jnp.int32, (rows, rows), 0)
    k = lax.broadcasted_iota(jnp.int32, (rows, rows), 1)
    before = jnp.where((k < j) & (k // block == j // block), 1.0, 0.0).astype(bf16)
    slot = nn(before, jnp.broadcast_to(mask, (rows, 128)).astype(bf16))[:, 0:1]
    j = lax.broadcasted_iota(jnp.int32, (rows, slots), 0)
    i = lax.broadcasted_iota(jnp.int32, (rows, slots), 1)
    target = slot.astype(jnp.int32) + CAP * (j // block)
    place = jnp.where((mask > 0.5) & (target == i), 1.0, 0.0).astype(bf16)
    place_ref[...] = place
    act_ref[...] = tn(place, act).astype(bf16)


def experts(info, near, far, w_in):
    slots = 16 * CAP
    return pl.pallas_call(
        expert_kernel,
        out_shape=[
            jax.ShapeDtypeStruct((slots, 128), bf16),
            jax.ShapeDtypeStruct((256, slots), bf16),
            jax.ShapeDtypeStruct((256, 1), f32),
        ],
        in_specs=[SMEM, VMEM, VMEM, pl.BlockSpec(memory_space=pltpu.HBM)],
        out_specs=[VMEM, VMEM, VMEM],
        scratch_shapes=[pltpu.VMEM(w_in.shape, bf16), pltpu.SemaphoreType.DMA((SIDE,))],
        compiler_params=pltpu.CompilerParams(vmem_limit_bytes=16 << 20),
    )(info, near, far, in_hbm(w_in))


def cut_down_kernel(info, w_hbm, o0, o1, o2, o3, w_ref, held, w_sem, sems):
    features = o0.shape[1]
    whole = pltpu.make_async_copy(w_hbm, w_ref, w_sem)
    whole.start()
    whole.wait()
    for place in range(SIDE):
        step = jnp.bitwise_xor(info[6], place)
        for square in range(SIDE):
            at = (NEIGHBOURS[place] + SQUARES[square]) * features
            held[step, square] = w_ref[:, at : at + features].T
    copies = [
        pltpu.make_async_copy(held.at[d], out, sems.at[d]) for d, out in enumerate((o0, o1, o2, o3))
    ]
    for copy in copies:
        copy.start()
    for copy in copies:
        copy.wait()


def cut_down(info, w_down, features):
    anywhere = pl.BlockSpec(memory_space=pltpu.HBM)
    shape = (SIDE, features, w_down.shape[0])
    return pl.pallas_call(
        cut_down_kernel,
        out_shape=[pltpu.HBM(shape, bf16)] * SIDE,
        in_specs=[SMEM, anywhere],
        out_specs=[anywhere] * SIDE,
        scratch_shapes=[
            pltpu.VMEM(w_down.shape, bf16),
            pltpu.VMEM((SIDE,) + shape, bf16),
            pltpu.SemaphoreType.DMA,
            pltpu.SemaphoreType.DMA((SIDE,)),
        ],
        compiler_params=pltpu.CompilerParams(vmem_limit_bytes=8 << 20),
    )(info, in_hbm(w_down))


def down_kernel(info, a0, a1, a2, a3, w0, w1, w2, w3, place_ref, gate_ref, near_ref, far_ref):
    place, gates = place_ref[...], gate_ref[...]
    half = near_ref.shape[1]
    for d in range(SIDE):
        to = jnp.bitwise_xor(info[7], d)
        total = sum(nt(a[...], w[to]) for a, w in ((a0, w0), (a1, w1), (a2, w2), (a3, w3)))
        high = total.astype(bf16)
        low = (total - high.astype(f32)).astype(bf16)
        share = (nn(place, high) + nn(place, low)) * gates
        near_ref[d] = share[:half]
        far_ref[d] = share[half:].astype(bf16)


def prompt_kernel(info, q_ref, keys_ref, out_ref, scores, weighted):
    pieces, tokens = keys_ref.shape[0], q_ref.shape[0]
    heads = q_ref.shape[1] // 576
    me, prefix_len = info[4], info[5]
    queries = jnp.concatenate([q_ref[:, h * 576 : (h + 1) * 576] for h in range(heads)], axis=0)
    rows = queries.shape[0]
    lane = lax.broadcasted_iota(jnp.int32, (tokens, 128), 1)
    ahead = lane - lax.broadcasted_iota(jnp.int32, (tokens, 128), 0)
    unroll = 8

    def score(i, top):
        for u in range(unroll):
            j = i * unroll + u
            early = jnp.where(lane < prefix_len - j * 128, 0.0, LOW)
            late = jnp.where(ahead <= (me - j) * tokens, 0.0, LOW)
            masks = jnp.concatenate([jnp.concatenate([early, late], axis=1)] * heads, axis=0)
            s = nn(queries, keys_ref[j]) + masks
            scores[j] = s
            top = jnp.maximum(top, jnp.maximum(s[:, :128], s[:, 128:]))
        return top

    top = lax.fori_loop(0, pieces // unroll, score, jnp.full((rows, 128), LOW, f32))
    top = jnp.max(top, axis=1, keepdims=True) * score_scale
    weighted[...] = jnp.zeros_like(weighted)

    def weigh(i, total):
        sums = jnp.zeros(weighted.shape, f32)
        for u in range(unroll):
            j = i * unroll + u
            p = jnp.exp(scores[j] * score_scale - top)
            total = total + (p[:, :128] + p[:, 128:])
            sums = sums + nt(p.astype(bf16), keys_ref[j, :LATENT])
        weighted[...] += sums
        return total

    total = lax.fori_loop(0, pieces // unroll, weigh, jnp.zeros((rows, 128), f32))
    total = jnp.sum(total, axis=1, keepdims=True)
    result = (weighted[...] / total).astype(bf16)
    for h in range(heads):
        out_ref[:, h * LATENT : (h + 1) * LATENT] = result[h * tokens : (h + 1) * tokens]


def prompt_attention(info, queries, keys, heads=4):
    tokens, width = queries.shape
    steps = width // (576 * heads)
    pieces = keys.shape[0]
    return pl.pallas_call(
        prompt_kernel,
        out_shape=jax.ShapeDtypeStruct((tokens, steps * heads * LATENT), bf16),
        grid=(steps,),
        in_specs=[
            SMEM,
            pl.BlockSpec((tokens, heads * 576), lambda i: (0, i)),
            pl.BlockSpec(keys.shape, lambda i: (0, 0, 0)),
        ],
        out_specs=pl.BlockSpec((tokens, heads * LATENT), lambda i: (0, i)),
        scratch_shapes=[
            pltpu.VMEM((pieces, heads * tokens, 256), f32),
            pltpu.VMEM((heads * tokens, LATENT), f32),
        ],
        compiler_params=pltpu.CompilerParams(vmem_limit_bytes=32 << 20),
        cost_estimate=pl.CostEstimate(
            flops=2 * 8 * tokens * 4096 * 1088, bytes_accessed=8 << 20, transcendentals=8 * tokens * 4096
        ),
    )(info, queries, keys)


def on_device(
    q_pre,
    prefix_cache,
    span_cache,
    prefix_len,
    q_dec,
    dec_cache,
    cache_len,
    requests,
    w_uv,
    w_out,
    x_dec,
    norm_gain,
    expert_ids,
    expert_gates,
    w_in,
    w_down,
):
    group = lax.axis_index("group")
    seq = lax.axis_index("seq")
    z = lax.axis_index("expert")
    shards = lax.axis_size("seq")
    depth = lax.axis_size("expert")
    info = jnp.stack(
        [
            group,
            seq // SIDE,
            seq % SIDE,
            group * depth + z,
            seq,
            prefix_len[0],
            seq % 2 + seq // SIDE % 2 * 2,
            seq // 2 % 2 + seq // (2 * SIDE) * 2,
        ]
    ).astype(jnp.int32)
    features = x_dec.shape[1]

    wanted = jnp.broadcast_to(requests.astype(bf16)[:, None], (8, 128))
    packet = jnp.concatenate(
        [
            jnp.concatenate([q_dec[:, : 4 * 576], wanted], axis=1),
            jnp.concatenate([q_dec[:, 4 * 576 :], wanted], axis=1),
        ],
        axis=0,
    )
    span, packet, prefix, columns = lax.optimization_barrier(
        (span_cache[0], packet, prefix_cache[0], span_cache[0])
    )
    keys = lax.all_gather(jnp.concatenate([prefix, columns], axis=1), "seq", axis=0)
    pieces, packets = along_x(span), along_y(packet)
    pieces, packets = lax.optimization_barrier((pieces, packets))
    resident, stacked = resident_attention(cache_len, packets[0], dec_cache, pieces)
    g_high = lax.reduce_precision(expert_gates, 8, 7)
    g_mid = lax.reduce_precision(expert_gates - g_high, 8, 7)
    g_low = lax.reduce_precision(expert_gates - g_high - g_mid, 8, 7)
    extra = jnp.concatenate(
        [expert_ids.astype(f32), g_high, g_mid, g_low, jnp.zeros((16, 32), f32)], axis=1
    )
    gain = lax.dynamic_slice(norm_gain, (seq * features,), (features,))[None]
    part = call(
        span_kernel,
        jax.ShapeDtypeStruct((32, 9 * VDIM), bf16),
        [info, *packets, *pieces, other_core(stacked), w_uv, resident],
        [pltpu.VMEM((SIDE, 8, 9 * VDIM), f32)],
        fetch=tuple(range(1, 11)),
        mib=16,
    )
    part, w_back = lax.optimization_barrier((part, w_down[0]))
    parts = along_y(part)
    w_back = cut_down(info, w_back, features)
    parts, w_back = lax.optimization_barrier((parts, w_back))
    *w_back, diagonal = [w_back[0]] + [swap(w_back[d], NEIGHBOURS[d]) for d in (1, 2)] + [w_back[3]]
    dec_val = call(
        merge_kernel,
        jax.ShapeDtypeStruct((32, 8 * VDIM), bf16),
        [info, *parts],
    )
    values = along_x(dec_val)
    product = call(
        project_kernel,
        jax.ShapeDtypeStruct((128, features), bf16),
        [info, *values, w_out.T],
        [pltpu.VMEM((SIDE, SIDE, 8, features), f32)],
    )
    terms = lax.all_to_all(product.reshape(depth, 16, features), "expert", 0, 0, tiled=True)

    hidden, packed = call(
        hidden_kernel,
        [
            jax.ShapeDtypeStruct((16, features), bf16),
            jax.ShapeDtypeStruct((16, features + 64), bf16),
        ],
        [info, terms, x_dec, gain, extra],
    )
    rows = everyone(packed, "expert", depth).reshape(16 * depth, features + 64)
    rows, q_pre, w_back = lax.optimization_barrier((rows, q_pre, w_back))
    arrived = everyone(rows, "seq", shards)
    o_pre = prompt_attention(info, q_pre[0], keys)[None]
    arrived, o_pre, diagonal = lax.optimization_barrier((arrived, o_pre, diagonal))
    w_back.append(swap(diagonal, NEIGHBOURS[3]))
    act, place, gate = experts(
        info, arrived, other_core(arrived), w_in[0].reshape(2, shards, features, 128)
    )
    shape = (SIDE, 16 * depth, features)
    near, far_share = call(
        down_kernel,
        [jax.ShapeDtypeStruct(shape, f32), jax.ShapeDtypeStruct(shape, bf16)],
        [info, act, *[swap(act, mask) for mask in NEIGHBOURS[1:]], *w_back, place, gate],
        mib=16,
    )
    share = (near + other_core(far_share).astype(f32)).astype(bf16)
    parts = [share[0]] + [swap(share[d], SQUARES[d]) for d in range(1, SIDE)]
    share = sum(v.astype(f32) for v in parts).astype(bf16)
    shares = lax.all_to_all(share.reshape(depth, 16, features), "expert", 0, 0, tiled=True)
    h_out = (hidden.astype(f32) + jnp.sum(shares.astype(f32), axis=0)).astype(bf16)

    return (o_pre, h_out)


def solution(mesh):
    return jax.shard_map(
        on_device,
        mesh=mesh,
        in_specs=(
            P("group", "seq", "expert"),
            P("group", None, "seq"),
            P("group", None, "seq"),
            P("group"),
            P(("group", "seq"), "expert"),
            P(("group", "seq"), None, None),
            P(("group", "seq")),
            P(("group", "seq")),
            P("expert", None, None),
            P("expert", "seq"),
            P(("group", "expert"), "seq"),
            P(),
            P(("group", "expert"), None),
            P(("group", "expert"), None),
            P(("group", "expert"), None, None, "seq"),
            P(("group", "expert"), "seq", None),
        ),
        out_specs=(P("group", "seq", "expert"), P(("group", "expert"), "seq")),
        check_vma=False,
    )
```

```python
import functools

import jax
import jax.numpy as jnp
from jax import lax
from jax.experimental import pallas as pl
from jax.experimental.pallas import tpu as pltpu
from jax.sharding import PartitionSpec as P

LATENT = 512
VDIM = 128
SIDE = 4
CAP = 12

ROWS_X = [[y * SIDE + x for x in range(SIDE)] for y in range(SIDE)]
ROWS_Y = [[y * SIDE + x for y in range(SIDE)] for x in range(SIDE)]

bf16 = jnp.bfloat16
f32 = jnp.float32
score_scale = 192.0 ** (-0.5)
epsilon = 1e-06
LOW = -1e30

VMEM = pl.BlockSpec(memory_space=pltpu.VMEM)
SMEM = pl.BlockSpec(memory_space=pltpu.SMEM)


def call(kernel, out_shape, ins, scratch=(), fetch=(), mib=8):
    multi = isinstance(out_shape, (tuple, list))

    def body(*refs):
        refs = list(refs)
        if fetch:
            held, sems = refs[-len(fetch) - 1 : -1], refs[-1]
            copies = [
                pltpu.make_async_copy(refs[at], to, sems.at[i])
                for i, (at, to) in enumerate(zip(fetch, held))
            ]
            for copy in copies:
                copy.start()
            for copy in copies:
                copy.wait()
            refs = refs[: -len(fetch) - 1]
            for at, to in zip(fetch, held):
                refs[at] = to
        kernel(*refs)

    held = [pltpu.VMEM(ins[at].shape, ins[at].dtype) for at in fetch]
    if fetch:
        held.append(pltpu.SemaphoreType.DMA((len(fetch),)))
    place = [SMEM] + [VMEM] * (len(ins) - 1)
    for at in fetch:
        place[at] = pl.BlockSpec(memory_space=pltpu.HBM)
    return pl.pallas_call(
        body,
        out_shape=out_shape,
        in_specs=place,
        out_specs=[VMEM] * len(out_shape) if multi else VMEM,
        scratch_shapes=list(scratch) + held,
        compiler_params=pltpu.CompilerParams(vmem_limit_bytes=mib << 20),
    )(*[in_hbm(v) if i in fetch else v for i, v in enumerate(ins)])


def in_hbm(array):
    return pltpu.with_memory_space_constraint(array, pltpu.HBM)


def in_vmem(array):
    return pltpu.with_memory_space_constraint(array, pltpu.VMEM)


def nn(a, b):
    return jnp.dot(a, b, preferred_element_type=f32)


def nt(a, b):
    return lax.dot_general(a, b, (((1,), (1,)), ((), ())), preferred_element_type=f32)


def tn(a, b):
    return lax.dot_general(a, b, (((0,), (0,)), ((), ())), preferred_element_type=f32)


def split3(v):
    high = v.astype(bf16).astype(f32)
    rest = v - high
    mid = rest.astype(bf16).astype(f32)
    return high, mid, (rest - mid).astype(bf16).astype(f32)


def to_x(array, d):
    return lax.ppermute(
        array,
        "seq",
        [(y * SIDE + x, y * SIDE + (x + d) % SIDE) for y in range(SIDE) for x in range(SIDE)],
    )


def to_y(array, d):
    return lax.ppermute(
        array,
        "seq",
        [(y * SIDE + x, (y + d) % SIDE * SIDE + x) for y in range(SIDE) for x in range(SIDE)],
    )


NEIGHBOURS = (0, 1, SIDE, SIDE + 1)
SQUARES = (0, 2, 2 * SIDE, 2 * SIDE + 2)


def swap(array, mask):
    return lax.ppermute(array, "seq", [(i, i ^ mask) for i in range(SIDE * SIDE)])


def along_x(array):
    return [array] + [to_x(array, d) for d in range(1, SIDE)]


def along_y(array):
    return [array] + [to_y(array, d) for d in range(1, SIDE)]


def other_core(array):
    return lax.ppermute(array, "group", [(0, 1), (1, 0)])


def everyone(array, axis, count, groups=None):
    return lax.all_to_all(
        jnp.broadcast_to(array[None], (count,) + array.shape),
        axis,
        0,
        0,
        tiled=True,
        axis_index_groups=groups,
    )


def head_rows(ref):
    raw = ref[...].astype(f32)
    heads = [raw[h // 4 * 8 : h // 4 * 8 + 8, h % 4 * 576 : h % 4 * 576 + 576] for h in range(8)]
    wanted = raw[:8, 4 * 576 : 4 * 576 + 1]
    return jnp.concatenate(heads, axis=0).astype(bf16), jnp.concatenate([wanted] * 8, axis=0)


def stack_kernel(k0, k1, k2, k3, out_ref):
    for d, k in enumerate((k0, k1, k2, k3)):
        out_ref[d] = k[...]


def stack_of(pieces):
    return pl.pallas_call(
        stack_kernel,
        out_shape=jax.ShapeDtypeStruct((SIDE,) + pieces[0].shape, bf16),
        in_specs=[VMEM] * SIDE,
        out_specs=VMEM,
        compiler_params=pltpu.CompilerParams(vmem_limit_bytes=4 << 20),
    )(*pieces)


def resident_kernel(lens, q_ref, cache_hbm, state_ref, cache_ref, sem):
    cache_copy = pltpu.make_async_copy(cache_hbm, cache_ref, sem)
    cache_copy.start()
    queries, _ = head_rows(q_ref)
    cache_copy.wait()
    count = cache_ref.shape[0]
    row = lax.rem(lax.broadcasted_iota(jnp.int32, (queries.shape[0], 128), 0), count)
    column = lax.broadcasted_iota(jnp.int32, (queries.shape[0], 128), 1)
    scores = []
    for r in range(count):
        s = nn(queries, cache_ref[r]) * score_scale
        scores.append(jnp.where((row == r) & (column < lens[r]), s, LOW))
    top = scores[0]
    for s in scores[1:]:
        top = jnp.maximum(top, s)
    m = jnp.max(top, axis=1, keepdims=True)
    total = jnp.zeros_like(top)
    weighted = jnp.zeros((queries.shape[0], LATENT), f32)
    for r in range(count):
        p = jnp.where((row == r) & (column < lens[r]), jnp.exp(scores[r] - m), 0.0)
        total += p
        weighted += nt(p.astype(bf16), cache_ref[r, :LATENT])
    state_ref[:, :LATENT] = weighted
    state_ref[:, LATENT : LATENT + 128] = jnp.broadcast_to(m, total.shape)
    state_ref[:, LATENT + 128 :] = jnp.broadcast_to(jnp.sum(total, axis=1, keepdims=True), total.shape)


def resident_attention(cache_len, packet, dec_cache):
    return pl.pallas_call(
        resident_kernel,
        out_shape=pltpu.VMEM((64, LATENT + 256), f32),
        in_specs=[SMEM, VMEM, pl.BlockSpec(memory_space=pltpu.HBM)],
        out_specs=VMEM,
        scratch_shapes=[pltpu.VMEM(dec_cache.shape, bf16), pltpu.SemaphoreType.DMA],
        compiler_params=pltpu.CompilerParams(vmem_limit_bytes=8 << 20),
    )(cache_len, packet, in_hbm(dec_cache))


def span_kernel(
    info, q0, q1, q2, q3, k0, k1, k2, k3, kp, w_uv, state, out_ref, scr
):
    group = info[0].astype(f32)
    y = info[1]
    parts = [head_rows(q) for q in (q0, q1, q2, q3)]
    queries = jnp.concatenate([p[0] for p in parts], axis=0)
    wanted = jnp.concatenate([p[1] for p in parts], axis=0)
    own_keys = jnp.concatenate([k0[...], k1[...], k2[...], k3[...]], axis=1)
    far_keys = jnp.concatenate([kp[0], kp[1], kp[2], kp[3]], axis=1)
    own = wanted == group
    valid = wanted < 1.5
    s = jnp.where(own, nn(queries, own_keys), nn(queries, far_keys)) * score_scale
    m = jnp.where(valid, jnp.max(s, axis=1, keepdims=True), LOW)
    p = jnp.where(valid, jnp.exp(s - m), 0.0)
    total = jnp.sum(p, axis=1, keepdims=True)
    weighted = nt(jnp.where(own, p, 0.0).astype(bf16), own_keys[:LATENT]) + nt(
        jnp.where(own, 0.0, p).astype(bf16), far_keys[:LATENT]
    )
    here = state.shape[0]
    rw = state[:, :LATENT]
    rm = state[:, LATENT : LATENT + 1]
    rl = state[:, LATENT + 128 : LATENT + 129]
    newest = jnp.maximum(m[:here], rm)
    a = jnp.exp(m[:here] - newest)
    b = jnp.exp(rm - newest)
    m = jnp.concatenate([newest, m[here:]], axis=0)
    total = jnp.concatenate([total[:here] * a + rl * b, total[here:]], axis=0)
    weighted = jnp.concatenate([weighted[:here] * a + rw * b, weighted[here:]], axis=0)
    some = total > 0.0
    safe = jnp.where(some, total, 1.0)
    latent = (weighted / safe).reshape(SIDE, 8, 8, LATENT)
    level = jnp.where(some, m + jnp.log(safe), LOW).reshape(SIDE, 8, 8, 1)
    lane = lax.broadcasted_iota(jnp.int32, (SIDE, 8, 128), 2)
    tail = jnp.zeros((SIDE, 8, 128), f32)
    places = [lax.rem(y - d + SIDE, SIDE) for d in range(SIDE)]
    for h in range(8):
        rows = latent[:, h].reshape(SIDE * 8, LATENT).astype(bf16)
        value = nn(rows, w_uv[h])
        for d in range(SIDE):
            scr[places[d], :, h * VDIM : (h + 1) * VDIM] = value[d * 8 : (d + 1) * 8]
        for part, v in enumerate(split3(level[:, h])):
            tail = jnp.where(lane == part * 8 + h, v, tail)
    for d in range(SIDE):
        scr[places[d], :, 8 * VDIM :] = tail[d]
    out_ref[...] = scr[...].reshape(SIDE * 8, 9 * VDIM).astype(bf16)


def merge_kernel(info, p0, p1, p2, p3, out_ref):
    parts = [p0, p1, p2, p3]
    levels = []
    for p in parts:
        tail = p[:, 8 * VDIM :].astype(f32)
        levels.append(tail[:, 0:8] + tail[:, 8:16] + tail[:, 16:24])
    top = functools.reduce(jnp.maximum, levels)
    weights = [jnp.exp(v - top) for v in levels]
    total = functools.reduce(jnp.add, weights)
    weights = [w / total for w in weights]
    for h in range(8):
        cut = slice(h * VDIM, (h + 1) * VDIM)
        value = sum(p[:, cut].astype(f32) * w[:, h : h + 1] for p, w in zip(parts, weights))
        out_ref[:, cut] = value.astype(bf16)


def project_kernel(info, x0, x1, x2, x3, w_out, out_ref, scr):
    x = info[2]
    rows = jnp.concatenate([x0[...], x1[...], x2[...], x3[...]], axis=0)
    product = nt(rows, w_out[...])
    for d in range(SIDE):
        place = lax.rem(x - d + SIDE, SIDE)
        for y in range(SIDE):
            at = (d * SIDE + y) * 8
            scr[y, place] = product[at : at + 8]
    out_ref[...] = scr[...].reshape(out_ref.shape).astype(bf16)


def hidden_kernel(info, terms_ref, x_ref, gain_ref, extra_ref, hidden_ref, packed_ref):
    attention = jnp.sum(terms_ref[...].astype(f32), axis=0)
    rounded = (x_ref[...].astype(f32) + attention).astype(bf16)
    hidden_ref[...] = rounded
    hidden = rounded.astype(f32)
    features = hidden.shape[1]
    gained = (hidden * gain_ref[...]).astype(bf16)
    extra = extra_ref[...]
    lane = lax.broadcasted_iota(jnp.int32, extra.shape, 1)
    for part, v in enumerate(split3(jnp.sum(hidden * hidden, axis=1, keepdims=True))):
        extra = jnp.where(lane == 32 + part, v, extra)
    extra = extra.astype(bf16)
    for i in range(packed_ref.shape[0]):
        packed_ref[i, :, :features] = gained
        packed_ref[i, :, features:] = extra


def products(x_ref, w_ref):
    shards, rows, _ = x_ref.shape
    features = w_ref.shape[2]
    both = jnp.zeros((rows, 256), f32)
    tails = jnp.zeros((rows, 64), f32)
    for s in range(shards):
        x = x_ref[s]
        both += nn(x[:, :features], jnp.concatenate([w_ref[0, s], w_ref[1, s]], axis=1))
        tails += x[:, features:].astype(f32)
    return both, tails


def near_kernel(info, near_ref, w_ref, both_ref, tails_ref):
    both_ref[...], tails_ref[...] = products(near_ref, w_ref)


def expert_kernel(info, near_ref, far_ref, w_ref, both_ref, tails_ref, act_ref, place_ref, gate_ref):
    shards, features, block = w_ref.shape[1], w_ref.shape[2], 16
    both, tails = products(far_ref, w_ref)
    both = jnp.concatenate([both_ref[...], both], axis=0)
    tails = jnp.concatenate([tails_ref[...], tails], axis=0)
    rows, slots = both.shape[0], act_ref.shape[0]
    squares = tails[:, 32:33] + tails[:, 33:34] + tails[:, 34:35]
    factor = lax.rsqrt(squares * (1.0 / (shards * features)) + epsilon)
    gate = both[:, :128] * factor
    act = (gate * (1.0 / (1.0 + jnp.exp(-gate))) * (both[:, 128:] * factor)).astype(bf16)
    extra = jnp.concatenate([near_ref[0, :, features:], far_ref[0, :, features:]], axis=0).astype(f32)
    hit = extra[:, 0:8] == info[3].astype(f32)
    mask = jnp.sum(jnp.where(hit, 1.0, 0.0), axis=1, keepdims=True)
    gates = extra[:, 8:16] + extra[:, 16:24] + extra[:, 24:32]
    gate_ref[...] = jnp.sum(jnp.where(hit, gates, 0.0), axis=1, keepdims=True)
    j = lax.broadcasted_iota(jnp.int32, (rows, rows), 0)
    k = lax.broadcasted_iota(jnp.int32, (rows, rows), 1)
    before = jnp.where((k < j) & (k // block == j // block), 1.0, 0.0).astype(bf16)
    slot = nn(before, jnp.broadcast_to(mask, (rows, 128)).astype(bf16))[:, 0:1]
    j = lax.broadcasted_iota(jnp.int32, (rows, slots), 0)
    i = lax.broadcasted_iota(jnp.int32, (rows, slots), 1)
    target = slot.astype(jnp.int32) + CAP * (j // block)
    place = jnp.where((mask > 0.5) & (target == i), 1.0, 0.0).astype(bf16)
    place_ref[...] = place
    act_ref[...] = tn(place, act).astype(bf16)


def experts(info, near, far, w_in):
    slots, rows = 16 * CAP, near.shape[1]
    both, tails = call(
        near_kernel,
        [jax.ShapeDtypeStruct((rows, 256), f32), jax.ShapeDtypeStruct((rows, 64), f32)],
        [info, near, w_in],
        mib=16,
    )
    return call(
        expert_kernel,
        [
            jax.ShapeDtypeStruct((slots, 128), bf16),
            jax.ShapeDtypeStruct((2 * rows, slots), bf16),
            jax.ShapeDtypeStruct((2 * rows, 1), f32),
        ],
        [info, near, far, w_in, both, tails],
        mib=16,
    )


def cut_down_kernel(info, w_ref, o0, o1, o2, o3, held, sems):
    features = o0.shape[1]
    for place in range(SIDE):
        step = jnp.bitwise_xor(info[6], place)
        for square in range(SIDE):
            at = (NEIGHBOURS[place] + SQUARES[square]) * features
            held[step, square] = w_ref[:, at : at + features].T
    copies = [
        pltpu.make_async_copy(held.at[d], out, sems.at[d]) for d, out in enumerate((o0, o1, o2, o3))
    ]
    for copy in copies:
        copy.start()
    for copy in copies:
        copy.wait()


def cut_down(info, w_down, features):
    anywhere = pl.BlockSpec(memory_space=pltpu.HBM)
    shape = (SIDE, features, w_down.shape[0])
    return pl.pallas_call(
        cut_down_kernel,
        out_shape=[pltpu.HBM(shape, bf16)] * SIDE,
        in_specs=[SMEM, VMEM],
        out_specs=[anywhere] * SIDE,
        scratch_shapes=[
            pltpu.VMEM((SIDE,) + shape, bf16),
            pltpu.SemaphoreType.DMA((SIDE,)),
        ],
        compiler_params=pltpu.CompilerParams(vmem_limit_bytes=8 << 20),
    )(info, w_down)


def down_kernel(info, a0, a1, a2, a3, w0, w1, w2, w3, place_ref, gate_ref, near_ref, far_ref):
    place, gates = place_ref[...], gate_ref[...]
    half = near_ref.shape[1]
    for square in range(SIDE):
        total = sum(nt(a[...], w[square]) for a, w in ((a0, w0), (a1, w1), (a2, w2), (a3, w3)))
        high = total.astype(bf16)
        low = (total - high.astype(f32)).astype(bf16)
        share = (nn(place, high) + nn(place, low)) * gates
        near_ref[square] = share[:half]
        far_ref[square] = share[half:].astype(bf16)


def prompt_kernel(info, q_ref, keys_hbm, out_ref, keys_ref, scores, weighted, sems):
    pieces, tokens = keys_ref.shape[0], q_ref.shape[0]
    step, unroll = pl.program_id(0), 8

    def fetch(i):
        part = pl.ds(i * unroll, unroll)
        return pltpu.make_async_copy(keys_hbm.at[part], keys_ref.at[part], sems.at[i])

    @pl.when(step == 0)
    def _():
        for i in range(pieces // unroll):
            fetch(i).start()

    heads = q_ref.shape[1] // 576
    me, prefix_len = info[4], info[5]
    queries = jnp.concatenate([q_ref[:, h * 576 : (h + 1) * 576] for h in range(heads)], axis=0)
    rows = queries.shape[0]
    lane = lax.broadcasted_iota(jnp.int32, (tokens, 128), 1)
    ahead = lane - lax.broadcasted_iota(jnp.int32, (tokens, 128), 0)

    def score(i, top):
        @pl.when(step == 0)
        def _():
            fetch(i).wait()

        for u in range(unroll):
            j = i * unroll + u
            early = jnp.where(lane < prefix_len - j * 128, 0.0, LOW)
            late = jnp.where(ahead <= (me - j) * tokens, 0.0, LOW)
            masks = jnp.concatenate([jnp.concatenate([early, late], axis=1)] * heads, axis=0)
            s = nn(queries, keys_ref[j]) + masks
            scores[j] = s
            top = jnp.maximum(top, jnp.maximum(s[:, :128], s[:, 128:]))
        return top

    top = lax.fori_loop(0, pieces // unroll, score, jnp.full((rows, 128), LOW, f32))
    top = jnp.max(top, axis=1, keepdims=True) * score_scale
    weighted[...] = jnp.zeros_like(weighted)

    def weigh(i, total):
        sums = jnp.zeros(weighted.shape, f32)
        for u in range(unroll):
            j = i * unroll + u
            p = jnp.exp(scores[j] * score_scale - top)
            total = total + (p[:, :128] + p[:, 128:])
            sums = sums + nt(p.astype(bf16), keys_ref[j, :LATENT])
        weighted[...] += sums
        return total

    total = lax.fori_loop(0, pieces // unroll, weigh, jnp.zeros((rows, 128), f32))
    total = jnp.sum(total, axis=1, keepdims=True)
    result = (weighted[...] / total).astype(bf16)
    for h in range(heads):
        out_ref[:, h * LATENT : (h + 1) * LATENT] = result[h * tokens : (h + 1) * tokens]

def prompt_attention(info, queries, keys, heads=4):
    tokens, width = queries.shape
    steps = width // (576 * heads)
    pieces = keys.shape[0]
    hbm = pl.BlockSpec(memory_space=pltpu.HBM)
    return pl.pallas_call(
        prompt_kernel,
        out_shape=jax.ShapeDtypeStruct((tokens, steps * heads * LATENT), bf16),
        grid=(steps,),
        in_specs=[SMEM, pl.BlockSpec((tokens, heads * 576), lambda i: (0, i)), hbm],
        out_specs=pl.BlockSpec((tokens, heads * LATENT), lambda i: (0, i)),
        scratch_shapes=[
            pltpu.VMEM(keys.shape, bf16),
            pltpu.VMEM((pieces, heads * tokens, 256), f32),
            pltpu.VMEM((heads * tokens, LATENT), f32),
            pltpu.SemaphoreType.DMA((pieces // 8,)),
        ],
        compiler_params=pltpu.CompilerParams(vmem_limit_bytes=32 << 20),
        cost_estimate=pl.CostEstimate(
            flops=2 * 8 * tokens * 4096 * 1088, bytes_accessed=8 << 20, transcendentals=8 * tokens * 4096
        ),
    )(info, in_hbm(queries), in_hbm(keys))


def on_device(
    q_pre,
    prefix_cache,
    span_cache,
    prefix_len,
    q_dec,
    dec_cache,
    cache_len,
    requests,
    w_uv,
    w_out,
    x_dec,
    norm_gain,
    expert_ids,
    expert_gates,
    w_in,
    w_down,
):
    group = lax.axis_index("group")
    seq = lax.axis_index("seq")
    z = lax.axis_index("expert")
    shards = lax.axis_size("seq")
    depth = lax.axis_size("expert")
    info = jnp.stack(
        [
            group,
            seq // SIDE,
            seq % SIDE,
            group * depth + z,
            seq,
            prefix_len[0],
            seq % 2 + seq // SIDE % 2 * 2,
            seq // 2 % 2 + seq // (2 * SIDE) * 2,
        ]
    ).astype(jnp.int32)
    features = x_dec.shape[1]

    wanted = jnp.broadcast_to(requests.astype(bf16)[:, None], (8, 128))
    packet = jnp.concatenate(
        [
            jnp.concatenate([q_dec[:, : 4 * 576], wanted], axis=1),
            jnp.concatenate([q_dec[:, 4 * 576 :], wanted], axis=1),
        ],
        axis=0,
    )
    span, packet, prefix, columns = lax.optimization_barrier(
        (span_cache[0], packet, prefix_cache[0], span_cache[0])
    )
    keys = lax.all_gather(jnp.concatenate([prefix, columns], axis=1), "seq", axis=0)
    pieces, packets = along_x(span), along_y(packet)
    pieces, packets = lax.optimization_barrier((pieces, packets))
    resident = resident_attention(cache_len, packets[0], dec_cache)
    g_high = lax.reduce_precision(expert_gates, 8, 7)
    g_mid = lax.reduce_precision(expert_gates - g_high, 8, 7)
    g_low = lax.reduce_precision(expert_gates - g_high - g_mid, 8, 7)
    extra = jnp.concatenate(
        [expert_ids.astype(f32), g_high, g_mid, g_low, jnp.zeros((16, 32), f32)], axis=1
    )
    gain = lax.dynamic_slice(norm_gain, (seq * features,), (features,))[None]
    part = call(
        span_kernel,
        jax.ShapeDtypeStruct((32, 9 * VDIM), bf16),
        [info, *packets, *pieces, other_core(stack_of(pieces)), w_uv, in_vmem(resident)],
        [pltpu.VMEM((SIDE, 8, 9 * VDIM), f32)],
        fetch=tuple(range(1, 11)),
        mib=16,
    )
    part, w_back = lax.optimization_barrier((part, w_down[0]))
    parts = along_y(part)
    w_back = cut_down(info, w_back, features)
    parts, w_back = lax.optimization_barrier((parts, w_back))
    *w_back, diagonal = [w_back[0]] + [swap(w_back[d], NEIGHBOURS[d]) for d in (1, 2)] + [w_back[3]]
    dec_val = call(
        merge_kernel,
        jax.ShapeDtypeStruct((32, 8 * VDIM), bf16),
        [info, *parts],
    )
    values = along_x(dec_val)
    product = call(
        project_kernel,
        jax.ShapeDtypeStruct((128, features), bf16),
        [info, *values, w_out.T],
        [pltpu.VMEM((SIDE, SIDE, 8, features), f32)],
    )
    terms = lax.all_to_all(product.reshape(depth, 16, features), "expert", 0, 0, tiled=True)

    hidden, packed = call(
        hidden_kernel,
        [
            jax.ShapeDtypeStruct((16, features), bf16),
            jax.ShapeDtypeStruct((depth, 16, features + 64), bf16),
        ],
        [info, terms, x_dec, gain, extra],
    )
    rows = lax.all_to_all(packed, "expert", 0, 0, tiled=True).reshape(16 * depth, features + 64)
    rows, q_pre, w_back = lax.optimization_barrier((rows, q_pre, w_back))
    arrived = everyone(rows, "seq", shards)
    o_pre = prompt_attention(info, q_pre[0], keys)
    arrived, o_pre, diagonal = lax.optimization_barrier((arrived, o_pre, diagonal))
    w_back.append(swap(diagonal, NEIGHBOURS[3]))
    act, place, gate = experts(
        info, arrived, other_core(arrived), w_in[0].reshape(2, shards, features, 128)
    )
    shape = (SIDE, 16 * depth, features)
    near, far_share = call(
        down_kernel,
        [jax.ShapeDtypeStruct(shape, f32), jax.ShapeDtypeStruct(shape, bf16)],
        [info, act, *[swap(act, mask) for mask in NEIGHBOURS[1:]], *w_back, place, gate],
        mib=16,
    )
    share = (near + other_core(far_share).astype(f32)).astype(bf16)
    same_place = [[place + square for square in SQUARES] for place in NEIGHBOURS]
    parts = lax.all_to_all(share, "seq", 0, 0, tiled=True, axis_index_groups=same_place)
    share = jnp.sum(parts.astype(f32), axis=0).astype(bf16)
    shares = lax.all_to_all(share.reshape(depth, 16, features), "expert", 0, 0, tiled=True)
    h_out = (hidden.astype(f32) + jnp.sum(shares.astype(f32), axis=0)).astype(bf16)

    return (o_pre[None], h_out)


def solution(mesh):
    return jax.shard_map(
        on_device,
        mesh=mesh,
        in_specs=(
            P("group", "seq", "expert"),
            P("group", None, "seq"),
            P("group", None, "seq"),
            P("group"),
            P(("group", "seq"), "expert"),
            P(("group", "seq"), None, None),
            P(("group", "seq")),
            P(("group", "seq")),
            P("expert", None, None),
            P("expert", "seq"),
            P(("group", "expert"), "seq"),
            P(),
            P(("group", "expert"), None),
            P(("group", "expert"), None),
            P(("group", "expert"), None, None, "seq"),
            P(("group", "expert"), "seq", None),
        ),
        out_specs=(P("group", "seq", "expert"), P(("group", "expert"), "seq")),
        check_vma=False,
    )
```

```python
import functools

import jax
import jax.numpy as jnp
from jax import lax
from jax.experimental import pallas as pl
from jax.experimental.pallas import tpu as pltpu
from jax.sharding import PartitionSpec as P

LATENT = 512
VDIM = 128
SIDE = 4
CAP = 12

ROWS_X = [[y * SIDE + x for x in range(SIDE)] for y in range(SIDE)]
ROWS_Y = [[y * SIDE + x for y in range(SIDE)] for x in range(SIDE)]

bf16 = jnp.bfloat16
f32 = jnp.float32
score_scale = 192.0 ** (-0.5)
epsilon = 1e-06
LOW = -1e30

VMEM = pl.BlockSpec(memory_space=pltpu.VMEM)
SMEM = pl.BlockSpec(memory_space=pltpu.SMEM)


def call(kernel, out_shape, ins, scratch=(), fetch=(), mib=8):
    multi = isinstance(out_shape, (tuple, list))

    def body(*refs):
        refs = list(refs)
        if fetch:
            held, sems = refs[-len(fetch) - 1 : -1], refs[-1]
            copies = [
                pltpu.make_async_copy(refs[at], to, sems.at[i])
                for i, (at, to) in enumerate(zip(fetch, held))
            ]
            for copy in copies:
                copy.start()
            for copy in copies:
                copy.wait()
            refs = refs[: -len(fetch) - 1]
            for at, to in zip(fetch, held):
                refs[at] = to
        kernel(*refs)

    held = [pltpu.VMEM(ins[at].shape, ins[at].dtype) for at in fetch]
    if fetch:
        held.append(pltpu.SemaphoreType.DMA((len(fetch),)))
    place = [SMEM] + [VMEM] * (len(ins) - 1)
    for at in fetch:
        place[at] = pl.BlockSpec(memory_space=pltpu.HBM)
    return pl.pallas_call(
        body,
        out_shape=out_shape,
        in_specs=place,
        out_specs=[VMEM] * len(out_shape) if multi else VMEM,
        scratch_shapes=list(scratch) + held,
        compiler_params=pltpu.CompilerParams(vmem_limit_bytes=mib << 20),
    )(*[in_hbm(v) if i in fetch else v for i, v in enumerate(ins)])


def in_hbm(array):
    return pltpu.with_memory_space_constraint(array, pltpu.HBM)


def in_vmem(array):
    return pltpu.with_memory_space_constraint(array, pltpu.VMEM)


def nn(a, b):
    return jnp.dot(a, b, preferred_element_type=f32)


def nt(a, b):
    return lax.dot_general(a, b, (((1,), (1,)), ((), ())), preferred_element_type=f32)


def tn(a, b):
    return lax.dot_general(a, b, (((0,), (0,)), ((), ())), preferred_element_type=f32)


def split3(v):
    high = v.astype(bf16).astype(f32)
    rest = v - high
    mid = rest.astype(bf16).astype(f32)
    return high, mid, (rest - mid).astype(bf16).astype(f32)


def to_x(array, d):
    return lax.ppermute(
        array,
        "seq",
        [(y * SIDE + x, y * SIDE + (x + d) % SIDE) for y in range(SIDE) for x in range(SIDE)],
    )


def to_y(array, d):
    return lax.ppermute(
        array,
        "seq",
        [(y * SIDE + x, (y + d) % SIDE * SIDE + x) for y in range(SIDE) for x in range(SIDE)],
    )


NEIGHBOURS = (0, 1, SIDE, SIDE + 1)
SQUARES = (0, 2, 2 * SIDE, 2 * SIDE + 2)


def swap(array, mask):
    return lax.ppermute(array, "seq", [(i, i ^ mask) for i in range(SIDE * SIDE)])


def along_x(array):
    return [array] + [to_x(array, d) for d in range(1, SIDE)]


def along_y(array):
    return [array] + [to_y(array, d) for d in range(1, SIDE)]


def other_core(array):
    return lax.ppermute(array, "group", [(0, 1), (1, 0)])


def everyone(array, axis, count, groups=None):
    return lax.all_to_all(
        jnp.broadcast_to(array[None], (count,) + array.shape),
        axis,
        0,
        0,
        tiled=True,
        axis_index_groups=groups,
    )


def head_rows(ref):
    raw = ref[...].astype(f32)
    heads = [raw[h // 4 * 8 : h // 4 * 8 + 8, h % 4 * 576 : h % 4 * 576 + 576] for h in range(8)]
    wanted = raw[:8, 4 * 576 : 4 * 576 + 1]
    return jnp.concatenate(heads, axis=0).astype(bf16), jnp.concatenate([wanted] * 8, axis=0)


def stack_kernel(k0, k1, k2, k3, out_ref, sem):
    own = pltpu.make_async_copy(k0, out_ref.at[0], sem)
    own.start()
    for d, k in enumerate((k1, k2, k3)):
        out_ref[d + 1] = k[...]
    own.wait()


def stack_of(pieces):
    return pl.pallas_call(
        stack_kernel,
        out_shape=pltpu.VMEM((SIDE,) + pieces[0].shape, bf16),
        in_specs=[pl.BlockSpec(memory_space=pltpu.HBM)] + [VMEM] * 3,
        out_specs=VMEM,
        scratch_shapes=[pltpu.SemaphoreType.DMA],
        compiler_params=pltpu.CompilerParams(vmem_limit_bytes=4 << 20),
    )(in_hbm(pieces[0]), *[in_vmem(piece) for piece in pieces[1:]])


def resident_kernel(lens, q_ref, cache_hbm, state_ref, cache_ref, sem):
    cache_copy = pltpu.make_async_copy(cache_hbm, cache_ref, sem)
    cache_copy.start()
    queries, _ = head_rows(q_ref)
    cache_copy.wait()
    count = cache_ref.shape[0]
    row = lax.rem(lax.broadcasted_iota(jnp.int32, (queries.shape[0], 128), 0), count)
    column = lax.broadcasted_iota(jnp.int32, (queries.shape[0], 128), 1)
    scores = []
    for r in range(count):
        s = nn(queries, cache_ref[r]) * score_scale
        scores.append(jnp.where((row == r) & (column < lens[r]), s, LOW))
    top = scores[0]
    for s in scores[1:]:
        top = jnp.maximum(top, s)
    m = jnp.max(top, axis=1, keepdims=True)
    total = jnp.zeros_like(top)
    weighted = jnp.zeros((queries.shape[0], LATENT), f32)
    for r in range(count):
        p = jnp.where((row == r) & (column < lens[r]), jnp.exp(scores[r] - m), 0.0)
        total += p
        weighted += nt(p.astype(bf16), cache_ref[r, :LATENT])
    state_ref[:, :LATENT] = weighted
    state_ref[:, LATENT : LATENT + 128] = jnp.broadcast_to(m, total.shape)
    state_ref[:, LATENT + 128 :] = jnp.broadcast_to(jnp.sum(total, axis=1, keepdims=True), total.shape)


def resident_attention(cache_len, packet, dec_cache):
    return pl.pallas_call(
        resident_kernel,
        out_shape=pltpu.VMEM((64, LATENT + 256), f32),
        in_specs=[SMEM, VMEM, pl.BlockSpec(memory_space=pltpu.HBM)],
        out_specs=VMEM,
        scratch_shapes=[pltpu.VMEM(dec_cache.shape, bf16), pltpu.SemaphoreType.DMA],
        compiler_params=pltpu.CompilerParams(vmem_limit_bytes=8 << 20),
    )(cache_len, packet, in_hbm(dec_cache))


def span_kernel(
    info, q0, q1, q2, q3, ko, kp, w_uv, state, out_ref, scr
):
    group = info[0].astype(f32)
    y = info[1]
    parts = [head_rows(q) for q in (q0, q1, q2, q3)]
    queries = jnp.concatenate([p[0] for p in parts], axis=0)
    wanted = jnp.concatenate([p[1] for p in parts], axis=0)
    own_keys = jnp.concatenate([ko[0], ko[1], ko[2], ko[3]], axis=1)
    far_keys = jnp.concatenate([kp[0], kp[1], kp[2], kp[3]], axis=1)
    own = wanted == group
    valid = wanted < 1.5
    s = jnp.where(own, nn(queries, own_keys), nn(queries, far_keys)) * score_scale
    m = jnp.where(valid, jnp.max(s, axis=1, keepdims=True), LOW)
    p = jnp.where(valid, jnp.exp(s - m), 0.0)
    total = jnp.sum(p, axis=1, keepdims=True)
    weighted = nt(jnp.where(own, p, 0.0).astype(bf16), own_keys[:LATENT]) + nt(
        jnp.where(own, 0.0, p).astype(bf16), far_keys[:LATENT]
    )
    here = state.shape[0]
    rw = state[:, :LATENT]
    rm = state[:, LATENT : LATENT + 1]
    rl = state[:, LATENT + 128 : LATENT + 129]
    newest = jnp.maximum(m[:here], rm)
    a = jnp.exp(m[:here] - newest)
    b = jnp.exp(rm - newest)
    m = jnp.concatenate([newest, m[here:]], axis=0)
    total = jnp.concatenate([total[:here] * a + rl * b, total[here:]], axis=0)
    weighted = jnp.concatenate([weighted[:here] * a + rw * b, weighted[here:]], axis=0)
    some = total > 0.0
    safe = jnp.where(some, total, 1.0)
    latent = (weighted / safe).reshape(SIDE, 8, 8, LATENT)
    level = jnp.where(some, m + jnp.log(safe), LOW).reshape(SIDE, 8, 8, 1)
    lane = lax.broadcasted_iota(jnp.int32, (SIDE, 8, 128), 2)
    tail = jnp.zeros((SIDE, 8, 128), f32)
    places = [lax.rem(y - d + SIDE, SIDE) for d in range(SIDE)]
    for h in range(8):
        rows = latent[:, h].reshape(SIDE * 8, LATENT).astype(bf16)
        value = nn(rows, w_uv[h])
        for d in range(SIDE):
            scr[places[d], :, h * VDIM : (h + 1) * VDIM] = value[d * 8 : (d + 1) * 8]
        for part, v in enumerate(split3(level[:, h])):
            tail = jnp.where(lane == part * 8 + h, v, tail)
    for d in range(SIDE):
        scr[places[d], :, 8 * VDIM :] = tail[d]
    out_ref[...] = scr[...].reshape(SIDE * 8, 9 * VDIM).astype(bf16)


def merge_kernel(info, p0, p1, p2, p3, out_ref):
    parts = [p0, p1, p2, p3]
    levels = []
    for p in parts:
        tail = p[:, 8 * VDIM :].astype(f32)
        levels.append(tail[:, 0:8] + tail[:, 8:16] + tail[:, 16:24])
    top = functools.reduce(jnp.maximum, levels)
    weights = [jnp.exp(v - top) for v in levels]
    total = functools.reduce(jnp.add, weights)
    weights = [w / total for w in weights]
    for h in range(8):
        cut = slice(h * VDIM, (h + 1) * VDIM)
        value = sum(p[:, cut].astype(f32) * w[:, h : h + 1] for p, w in zip(parts, weights))
        out_ref[:, cut] = value.astype(bf16)


def project_kernel(info, x0, x1, x2, x3, w_out, out_ref, scr):
    x = info[2]
    rows = jnp.concatenate([x0[...], x1[...], x2[...], x3[...]], axis=0)
    product = nt(rows, w_out[...])
    for d in range(SIDE):
        place = lax.rem(x - d + SIDE, SIDE)
        for y in range(SIDE):
            at = (d * SIDE + y) * 8
            scr[y, place] = product[at : at + 8]
    out_ref[...] = scr[...].reshape(out_ref.shape).astype(bf16)


def hidden_kernel(info, terms_ref, x_ref, gain_ref, ids_ref, gates_ref, hidden_ref, packed_ref):
    attention = jnp.sum(terms_ref[...].astype(f32), axis=0)
    rounded = (x_ref[...].astype(f32) + attention).astype(bf16)
    hidden_ref[...] = rounded
    hidden = rounded.astype(f32)
    features = hidden.shape[1]
    gained = (hidden * gain_ref[...]).astype(bf16)
    columns = [ids_ref[...].astype(f32), *split3(gates_ref[...])]
    columns += split3(jnp.sum(hidden * hidden, axis=1, keepdims=True))
    extra = jnp.concatenate([*columns, jnp.zeros((hidden.shape[0], 29), f32)], axis=1)
    extra = extra.astype(bf16)
    for i in range(packed_ref.shape[0]):
        packed_ref[i, :, :features] = gained
        packed_ref[i, :, features:] = extra


def products(x_ref, w_ref):
    shards, rows, _ = x_ref.shape
    features = w_ref.shape[2]
    both = jnp.zeros((rows, 256), f32)
    tails = jnp.zeros((rows, 64), f32)
    for s in range(shards):
        x = x_ref[s]
        both += nn(x[:, :features], jnp.concatenate([w_ref[0, s], w_ref[1, s]], axis=1))
        tails += x[:, features:].astype(f32)
    return both, tails


def near_kernel(info, near_ref, w_ref, both_ref, tails_ref):
    both_ref[...], tails_ref[...] = products(near_ref, w_ref)


def expert_kernel(info, near_ref, far_ref, w_ref, both_ref, tails_ref, act_ref, place_ref, gate_ref):
    shards, features, block = w_ref.shape[1], w_ref.shape[2], 16
    both, tails = products(far_ref, w_ref)
    both = jnp.concatenate([both_ref[...], both], axis=0)
    tails = jnp.concatenate([tails_ref[...], tails], axis=0)
    rows, slots = both.shape[0], act_ref.shape[0]
    squares = tails[:, 32:33] + tails[:, 33:34] + tails[:, 34:35]
    factor = lax.rsqrt(squares * (1.0 / (shards * features)) + epsilon)
    gate = both[:, :128] * factor
    act = (gate * (1.0 / (1.0 + jnp.exp(-gate))) * (both[:, 128:] * factor)).astype(bf16)
    extra = jnp.concatenate([near_ref[0, :, features:], far_ref[0, :, features:]], axis=0).astype(f32)
    hit = extra[:, 0:8] == info[3].astype(f32)
    mask = jnp.sum(jnp.where(hit, 1.0, 0.0), axis=1, keepdims=True)
    gates = extra[:, 8:16] + extra[:, 16:24] + extra[:, 24:32]
    gate_ref[...] = jnp.sum(jnp.where(hit, gates, 0.0), axis=1, keepdims=True)
    j = lax.broadcasted_iota(jnp.int32, (rows, rows), 0)
    k = lax.broadcasted_iota(jnp.int32, (rows, rows), 1)
    before = jnp.where((k < j) & (k // block == j // block), 1.0, 0.0).astype(bf16)
    slot = nn(before, jnp.broadcast_to(mask, (rows, 128)).astype(bf16))[:, 0:1]
    j = lax.broadcasted_iota(jnp.int32, (rows, slots), 0)
    i = lax.broadcasted_iota(jnp.int32, (rows, slots), 1)
    target = slot.astype(jnp.int32) + CAP * (j // block)
    place = jnp.where((mask > 0.5) & (target == i), 1.0, 0.0).astype(bf16)
    place_ref[...] = place
    act_ref[...] = tn(place, act).astype(bf16)


def experts(info, near, far, w_in):
    slots, rows = 16 * CAP, near.shape[1]
    both, tails = call(
        near_kernel,
        [jax.ShapeDtypeStruct((rows, 256), f32), jax.ShapeDtypeStruct((rows, 64), f32)],
        [info, near, w_in],
        mib=16,
    )
    return call(
        expert_kernel,
        [
            jax.ShapeDtypeStruct((slots, 128), bf16),
            jax.ShapeDtypeStruct((2 * rows, slots), bf16),
            jax.ShapeDtypeStruct((2 * rows, 1), f32),
        ],
        [info, near, far, w_in, both, tails],
        mib=16,
    )


def cut_down_kernel(info, w_ref, o0, o1, o2, o3, held, sems):
    features = o0.shape[1]
    for place in range(SIDE):
        step = jnp.bitwise_xor(info[6], place)
        for square in range(SIDE):
            at = (NEIGHBOURS[place] + SQUARES[square]) * features
            held[step, square] = w_ref[:, at : at + features].T
    copies = [
        pltpu.make_async_copy(held.at[d], out, sems.at[d]) for d, out in enumerate((o0, o1, o2, o3))
    ]
    for copy in copies:
        copy.start()
    for copy in copies:
        copy.wait()


def cut_down(info, w_down, features):
    anywhere = pl.BlockSpec(memory_space=pltpu.HBM)
    shape = (SIDE, features, w_down.shape[0])
    return pl.pallas_call(
        cut_down_kernel,
        out_shape=[pltpu.HBM(shape, bf16)] * SIDE,
        in_specs=[SMEM, VMEM],
        out_specs=[anywhere] * SIDE,
        scratch_shapes=[
            pltpu.VMEM((SIDE,) + shape, bf16),
            pltpu.SemaphoreType.DMA((SIDE,)),
        ],
        compiler_params=pltpu.CompilerParams(vmem_limit_bytes=8 << 20),
    )(info, w_down)


def down_kernel(info, a0, a1, a2, a3, w0, w1, w2, w3, place_ref, gate_ref, near_ref, far_ref):
    place, gates = place_ref[...], gate_ref[...]
    half = near_ref.shape[1]
    for square in range(SIDE):
        total = sum(nt(a[...], w[square]) for a, w in ((a0, w0), (a1, w1), (a2, w2), (a3, w3)))
        high = total.astype(bf16)
        low = (total - high.astype(f32)).astype(bf16)
        share = (nn(place, high) + nn(place, low)) * gates
        near_ref[square] = share[:half]
        far_ref[square] = share[half:].astype(bf16)


def prompt_kernel(info, q_ref, keys_hbm, out_ref, keys_ref, scores, weighted, sems):
    pieces, tokens = keys_ref.shape[0], q_ref.shape[0]
    step, unroll = pl.program_id(0), 8

    def fetch(i):
        part = pl.ds(i * unroll, unroll)
        return pltpu.make_async_copy(keys_hbm.at[part], keys_ref.at[part], sems.at[i])

    @pl.when(step == 0)
    def _():
        for i in range(pieces // unroll):
            fetch(i).start()

    heads = q_ref.shape[1] // 576
    me, prefix_len = info[4], info[5]
    queries = jnp.concatenate([q_ref[:, h * 576 : (h + 1) * 576] for h in range(heads)], axis=0)
    rows = queries.shape[0]
    lane = lax.broadcasted_iota(jnp.int32, (tokens, 128), 1)
    ahead = lane - lax.broadcasted_iota(jnp.int32, (tokens, 128), 0)

    def score(i, top):
        @pl.when(step == 0)
        def _():
            fetch(i).wait()

        for u in range(unroll):
            j = i * unroll + u
            early = jnp.where(lane < prefix_len - j * 128, 0.0, LOW)
            late = jnp.where(ahead <= (me - j) * tokens, 0.0, LOW)
            masks = jnp.concatenate([jnp.concatenate([early, late], axis=1)] * heads, axis=0)
            s = nn(queries, keys_ref[j]) + masks
            scores[j] = s
            top = jnp.maximum(top, jnp.maximum(s[:, :128], s[:, 128:]))
        return top

    top = lax.fori_loop(0, pieces // unroll, score, jnp.full((rows, 128), LOW, f32))
    top = jnp.max(top, axis=1, keepdims=True) * score_scale
    weighted[...] = jnp.zeros_like(weighted)

    def weigh(i, total):
        sums = jnp.zeros(weighted.shape, f32)
        for u in range(unroll):
            j = i * unroll + u
            p = jnp.exp(scores[j] * score_scale - top)
            total = total + (p[:, :128] + p[:, 128:])
            sums = sums + nt(p.astype(bf16), keys_ref[j, :LATENT])
        weighted[...] += sums
        return total

    total = lax.fori_loop(0, pieces // unroll, weigh, jnp.zeros((rows, 128), f32))
    total = jnp.sum(total, axis=1, keepdims=True)
    result = (weighted[...] / total).astype(bf16)
    for h in range(heads):
        out_ref[:, h * LATENT : (h + 1) * LATENT] = result[h * tokens : (h + 1) * tokens]

def prompt_attention(info, queries, keys, heads=4):
    tokens, width = queries.shape
    steps = width // (576 * heads)
    pieces = keys.shape[0]
    hbm = pl.BlockSpec(memory_space=pltpu.HBM)
    return pl.pallas_call(
        prompt_kernel,
        out_shape=jax.ShapeDtypeStruct((tokens, steps * heads * LATENT), bf16),
        grid=(steps,),
        in_specs=[SMEM, pl.BlockSpec((tokens, heads * 576), lambda i: (0, i)), hbm],
        out_specs=pl.BlockSpec((tokens, heads * LATENT), lambda i: (0, i)),
        scratch_shapes=[
            pltpu.VMEM(keys.shape, bf16),
            pltpu.VMEM((pieces, heads * tokens, 256), f32),
            pltpu.VMEM((heads * tokens, LATENT), f32),
            pltpu.SemaphoreType.DMA((pieces // 8,)),
        ],
        compiler_params=pltpu.CompilerParams(vmem_limit_bytes=32 << 20),
        cost_estimate=pl.CostEstimate(
            flops=2 * 8 * tokens * 4096 * 1088, bytes_accessed=8 << 20, transcendentals=8 * tokens * 4096
        ),
    )(info, in_hbm(queries), in_hbm(keys))


def on_device(
    q_pre,
    prefix_cache,
    span_cache,
    prefix_len,
    q_dec,
    dec_cache,
    cache_len,
    requests,
    w_uv,
    w_out,
    x_dec,
    norm_gain,
    expert_ids,
    expert_gates,
    w_in,
    w_down,
):
    group = lax.axis_index("group")
    seq = lax.axis_index("seq")
    z = lax.axis_index("expert")
    shards = lax.axis_size("seq")
    depth = lax.axis_size("expert")
    info = jnp.stack(
        [
            group,
            seq // SIDE,
            seq % SIDE,
            group * depth + z,
            seq,
            prefix_len[0],
            seq % 2 + seq // SIDE % 2 * 2,
            seq // 2 % 2 + seq // (2 * SIDE) * 2,
        ]
    ).astype(jnp.int32)
    features = x_dec.shape[1]

    wanted = jnp.broadcast_to(requests.astype(bf16)[:, None], (8, 128))
    packet = jnp.concatenate(
        [
            jnp.concatenate([q_dec[:, : 4 * 576], wanted], axis=1),
            jnp.concatenate([q_dec[:, 4 * 576 :], wanted], axis=1),
        ],
        axis=0,
    )
    span, packet, prefix, columns = lax.optimization_barrier(
        (span_cache[0], packet, prefix_cache[0], span_cache[0])
    )
    keys = lax.all_gather(jnp.concatenate([prefix, columns], axis=1), "seq", axis=0)
    pieces, packets = along_x(span), along_y(packet)
    pieces, packets = lax.optimization_barrier((pieces, packets))
    resident = resident_attention(cache_len, packets[0], dec_cache)
    stacked = stack_of(pieces)
    part = call(
        span_kernel,
        jax.ShapeDtypeStruct((32, 9 * VDIM), bf16),
        [info, *[in_vmem(v) for v in (*packets, stacked, other_core(stacked))], w_uv, in_vmem(resident)],
        [pltpu.VMEM((SIDE, 8, 9 * VDIM), f32)],
        fetch=(7,),
        mib=16,
    )
    part, w_back = lax.optimization_barrier((part, w_down[0]))
    parts = along_y(part)
    w_back = cut_down(info, w_back, features)
    parts, w_back = lax.optimization_barrier((parts, w_back))
    *w_back, diagonal = [w_back[0]] + [swap(w_back[d], NEIGHBOURS[d]) for d in (1, 2)] + [w_back[3]]
    dec_val = call(
        merge_kernel,
        jax.ShapeDtypeStruct((32, 8 * VDIM), bf16),
        [info, *parts],
    )
    values = along_x(dec_val)
    product = call(
        project_kernel,
        jax.ShapeDtypeStruct((128, features), bf16),
        [info, *values, w_out.T],
        [pltpu.VMEM((SIDE, SIDE, 8, features), f32)],
    )
    product, expert_ids, expert_gates, norm_gain, x_dec = lax.optimization_barrier(
        (product, expert_ids, expert_gates, norm_gain, x_dec)
    )
    terms = lax.all_to_all(product.reshape(depth, 16, features), "expert", 0, 0, tiled=True)

    gain = lax.dynamic_slice(norm_gain, (seq * features,), (features,))[None]
    hidden, packed = call(
        hidden_kernel,
        [
            jax.ShapeDtypeStruct((16, features), bf16),
            jax.ShapeDtypeStruct((depth, 16, features + 64), bf16),
        ],
        [info, terms, x_dec, gain, expert_ids, expert_gates],
    )
    rows = lax.all_to_all(packed, "expert", 0, 0, tiled=True).reshape(16 * depth, features + 64)
    rows, q_pre, w_back = lax.optimization_barrier((rows, q_pre, w_back))
    arrived = everyone(rows, "seq", shards)
    o_pre = prompt_attention(info, q_pre[0], keys)
    arrived, o_pre, diagonal = lax.optimization_barrier((arrived, o_pre, diagonal))
    w_back.append(swap(diagonal, NEIGHBOURS[3]))
    act, place, gate = experts(
        info, arrived, other_core(arrived), w_in[0].reshape(2, shards, features, 128)
    )
    shape = (SIDE, 16 * depth, features)
    near, far_share = call(
        down_kernel,
        [jax.ShapeDtypeStruct(shape, f32), jax.ShapeDtypeStruct(shape, bf16)],
        [info, act, *[swap(act, mask) for mask in NEIGHBOURS[1:]], *w_back, place, gate],
        mib=16,
    )
    share = (near + other_core(far_share).astype(f32)).astype(bf16)
    same_place = [[place + square for square in SQUARES] for place in NEIGHBOURS]
    parts = lax.all_to_all(share, "seq", 0, 0, tiled=True, axis_index_groups=same_place)
    share = jnp.sum(parts.astype(f32), axis=0).astype(bf16)
    shares = lax.all_to_all(share.reshape(depth, 16, features), "expert", 0, 0, tiled=True)
    h_out = (hidden.astype(f32) + jnp.sum(shares.astype(f32), axis=0)).astype(bf16)

    return (o_pre[None], h_out)


def solution(mesh):
    return jax.shard_map(
        on_device,
        mesh=mesh,
        in_specs=(
            P("group", "seq", "expert"),
            P("group", None, "seq"),
            P("group", None, "seq"),
            P("group"),
            P(("group", "seq"), "expert"),
            P(("group", "seq"), None, None),
            P(("group", "seq")),
            P(("group", "seq")),
            P("expert", None, None),
            P("expert", "seq"),
            P(("group", "expert"), "seq"),
            P(),
            P(("group", "expert"), None),
            P(("group", "expert"), None),
            P(("group", "expert"), None, None, "seq"),
            P(("group", "expert"), "seq", None),
        ),
        out_specs=(P("group", "seq", "expert"), P(("group", "expert"), "seq")),
        check_vma=False,
    )
```

```python
import functools

import jax
import jax.numpy as jnp
from jax import lax
from jax.experimental import pallas as pl
from jax.experimental.pallas import tpu as pltpu
from jax.sharding import PartitionSpec as P

LATENT = 512
VDIM = 128
SIDE = 4
CAP = 12

ROWS_X = [[y * SIDE + x for x in range(SIDE)] for y in range(SIDE)]
ROWS_Y = [[y * SIDE + x for y in range(SIDE)] for x in range(SIDE)]

bf16 = jnp.bfloat16
f32 = jnp.float32
score_scale = 192.0 ** (-0.5)
epsilon = 1e-06
LOW = -1e30

VMEM = pl.BlockSpec(memory_space=pltpu.VMEM)
SMEM = pl.BlockSpec(memory_space=pltpu.SMEM)


def call(kernel, out_shape, ins, scratch=(), fetch=(), mib=8):
    multi = isinstance(out_shape, (tuple, list))

    def body(*refs):
        refs = list(refs)
        if fetch:
            held, sems = refs[-len(fetch) - 1 : -1], refs[-1]
            copies = [
                pltpu.make_async_copy(refs[at], to, sems.at[i])
                for i, (at, to) in enumerate(zip(fetch, held))
            ]
            for copy in copies:
                copy.start()
            for copy in copies:
                copy.wait()
            refs = refs[: -len(fetch) - 1]
            for at, to in zip(fetch, held):
                refs[at] = to
        kernel(*refs)

    held = [pltpu.VMEM(ins[at].shape, ins[at].dtype) for at in fetch]
    if fetch:
        held.append(pltpu.SemaphoreType.DMA((len(fetch),)))
    place = [SMEM] + [VMEM] * (len(ins) - 1)
    for at in fetch:
        place[at] = pl.BlockSpec(memory_space=pltpu.HBM)
    return pl.pallas_call(
        body,
        out_shape=out_shape,
        in_specs=place,
        out_specs=[VMEM] * len(out_shape) if multi else VMEM,
        scratch_shapes=list(scratch) + held,
        compiler_params=pltpu.CompilerParams(vmem_limit_bytes=mib << 20),
    )(*[in_hbm(v) if i in fetch else v for i, v in enumerate(ins)])


def in_hbm(array):
    return pltpu.with_memory_space_constraint(array, pltpu.HBM)


def in_vmem(array):
    return pltpu.with_memory_space_constraint(array, pltpu.VMEM)


def nn(a, b):
    return jnp.dot(a, b, preferred_element_type=f32)


def nt(a, b):
    return lax.dot_general(a, b, (((1,), (1,)), ((), ())), preferred_element_type=f32)


def tn(a, b):
    return lax.dot_general(a, b, (((0,), (0,)), ((), ())), preferred_element_type=f32)


def split3(v):
    high = v.astype(bf16).astype(f32)
    rest = v - high
    mid = rest.astype(bf16).astype(f32)
    return high, mid, (rest - mid).astype(bf16).astype(f32)


def to_x(array, d):
    return lax.ppermute(
        array,
        "seq",
        [(y * SIDE + x, y * SIDE + (x + d) % SIDE) for y in range(SIDE) for x in range(SIDE)],
    )


def to_y(array, d):
    return lax.ppermute(
        array,
        "seq",
        [(y * SIDE + x, (y + d) % SIDE * SIDE + x) for y in range(SIDE) for x in range(SIDE)],
    )


NEIGHBOURS = (0, 1, SIDE, SIDE + 1)
SQUARES = (0, 2, 2 * SIDE, 2 * SIDE + 2)


def swap(array, mask):
    return lax.ppermute(array, "seq", [(i, i ^ mask) for i in range(SIDE * SIDE)])


def along_x(array):
    return [array] + [to_x(array, d) for d in range(1, SIDE)]


def along_y(array):
    return [array] + [to_y(array, d) for d in range(1, SIDE)]


def other_core(array):
    return lax.ppermute(array, "group", [(0, 1), (1, 0)])


def everyone(array, axis, count, groups=None):
    return lax.all_to_all(
        jnp.broadcast_to(array[None], (count,) + array.shape),
        axis,
        0,
        0,
        tiled=True,
        axis_index_groups=groups,
    )


def head_rows(ref):
    raw = ref[...].astype(f32)
    heads = [raw[h // 4 * 8 : h // 4 * 8 + 8, h % 4 * 576 : h % 4 * 576 + 576] for h in range(8)]
    wanted = raw[:8, 4 * 576 : 4 * 576 + 1]
    return jnp.concatenate(heads, axis=0).astype(bf16), jnp.concatenate([wanted] * 8, axis=0)


def stack_kernel(k0, k1, k2, k3, out_ref, sem):
    own = pltpu.make_async_copy(k0, out_ref.at[0], sem)
    own.start()
    for d, k in enumerate((k1, k2, k3)):
        out_ref[d + 1] = k[...]
    own.wait()


def stack_of(pieces):
    return pl.pallas_call(
        stack_kernel,
        out_shape=pltpu.VMEM((SIDE,) + pieces[0].shape, bf16),
        in_specs=[pl.BlockSpec(memory_space=pltpu.HBM)] + [VMEM] * 3,
        out_specs=VMEM,
        scratch_shapes=[pltpu.SemaphoreType.DMA],
        compiler_params=pltpu.CompilerParams(vmem_limit_bytes=4 << 20),
    )(in_hbm(pieces[0]), *[in_vmem(piece) for piece in pieces[1:]])


def resident_kernel(lens, q_ref, cache_ref, state_ref):
    queries, _ = head_rows(q_ref)
    count = cache_ref.shape[0]
    row = lax.rem(lax.broadcasted_iota(jnp.int32, (queries.shape[0], 128), 0), count)
    column = lax.broadcasted_iota(jnp.int32, (queries.shape[0], 128), 1)
    scores = []
    for r in range(count):
        s = nn(queries, cache_ref[r]) * score_scale
        scores.append(jnp.where((row == r) & (column < lens[r]), s, LOW))
    top = scores[0]
    for s in scores[1:]:
        top = jnp.maximum(top, s)
    m = jnp.max(top, axis=1, keepdims=True)
    total = jnp.zeros_like(top)
    weighted = jnp.zeros((queries.shape[0], LATENT), f32)
    for r in range(count):
        p = jnp.where((row == r) & (column < lens[r]), jnp.exp(scores[r] - m), 0.0)
        total += p
        weighted += nt(p.astype(bf16), cache_ref[r, :LATENT])
    state_ref[:, :LATENT] = weighted
    state_ref[:, LATENT : LATENT + 128] = jnp.broadcast_to(m, total.shape)
    state_ref[:, LATENT + 128 :] = jnp.broadcast_to(jnp.sum(total, axis=1, keepdims=True), total.shape)


def resident_attention(cache_len, packet, dec_cache):
    return pl.pallas_call(
        resident_kernel,
        out_shape=pltpu.VMEM((64, LATENT + 256), f32),
        in_specs=[SMEM, VMEM, VMEM],
        out_specs=VMEM,
        compiler_params=pltpu.CompilerParams(vmem_limit_bytes=8 << 20),
    )(cache_len, packet, in_vmem(dec_cache))


def span_kernel(
    info, q0, q1, q2, q3, ko, kp, w_uv, state, out_ref, scr
):
    group = info[0].astype(f32)
    y = info[1]
    parts = [head_rows(q) for q in (q0, q1, q2, q3)]
    queries = jnp.concatenate([p[0] for p in parts], axis=0)
    wanted = jnp.concatenate([p[1] for p in parts], axis=0)
    own_keys = jnp.concatenate([ko[0], ko[1], ko[2], ko[3]], axis=1)
    far_keys = jnp.concatenate([kp[0], kp[1], kp[2], kp[3]], axis=1)
    own = wanted == group
    valid = wanted < 1.5
    s = jnp.where(own, nn(queries, own_keys), nn(queries, far_keys)) * score_scale
    m = jnp.where(valid, jnp.max(s, axis=1, keepdims=True), LOW)
    p = jnp.where(valid, jnp.exp(s - m), 0.0)
    total = jnp.sum(p, axis=1, keepdims=True)
    weighted = nt(jnp.where(own, p, 0.0).astype(bf16), own_keys[:LATENT]) + nt(
        jnp.where(own, 0.0, p).astype(bf16), far_keys[:LATENT]
    )
    here = state.shape[0]
    rw = state[:, :LATENT]
    rm = state[:, LATENT : LATENT + 1]
    rl = state[:, LATENT + 128 : LATENT + 129]
    newest = jnp.maximum(m[:here], rm)
    a = jnp.exp(m[:here] - newest)
    b = jnp.exp(rm - newest)
    m = jnp.concatenate([newest, m[here:]], axis=0)
    total = jnp.concatenate([total[:here] * a + rl * b, total[here:]], axis=0)
    weighted = jnp.concatenate([weighted[:here] * a + rw * b, weighted[here:]], axis=0)
    some = total > 0.0
    safe = jnp.where(some, total, 1.0)
    latent = (weighted / safe).reshape(SIDE, 8, 8, LATENT)
    level = jnp.where(some, m + jnp.log(safe), LOW).reshape(SIDE, 8, 8, 1)
    lane = lax.broadcasted_iota(jnp.int32, (SIDE, 8, 128), 2)
    tail = jnp.zeros((SIDE, 8, 128), f32)
    places = [lax.rem(y - d + SIDE, SIDE) for d in range(SIDE)]
    for h in range(8):
        rows = latent[:, h].reshape(SIDE * 8, LATENT).astype(bf16)
        value = nn(rows, w_uv[h])
        for d in range(SIDE):
            scr[places[d], :, h * VDIM : (h + 1) * VDIM] = value[d * 8 : (d + 1) * 8]
        for part, v in enumerate(split3(level[:, h])):
            tail = jnp.where(lane == part * 8 + h, v, tail)
    for d in range(SIDE):
        scr[places[d], :, 8 * VDIM :] = tail[d]
    out_ref[...] = scr[...].reshape(SIDE * 8, 9 * VDIM).astype(bf16)


def merge_kernel(info, p0, p1, p2, p3, out_ref):
    parts = [p0, p1, p2, p3]
    levels = []
    for p in parts:
        tail = p[:, 8 * VDIM :].astype(f32)
        levels.append(tail[:, 0:8] + tail[:, 8:16] + tail[:, 16:24])
    top = functools.reduce(jnp.maximum, levels)
    weights = [jnp.exp(v - top) for v in levels]
    total = functools.reduce(jnp.add, weights)
    weights = [w / total for w in weights]
    for h in range(8):
        cut = slice(h * VDIM, (h + 1) * VDIM)
        value = sum(p[:, cut].astype(f32) * w[:, h : h + 1] for p, w in zip(parts, weights))
        out_ref[:, cut] = value.astype(bf16)


def project_kernel(info, x0, x1, x2, x3, w_out, out_ref, scr):
    x = info[2]
    rows = jnp.concatenate([x0[...], x1[...], x2[...], x3[...]], axis=0)
    product = nt(rows, w_out[...])
    for d in range(SIDE):
        place = lax.rem(x - d + SIDE, SIDE)
        for y in range(SIDE):
            at = (d * SIDE + y) * 8
            scr[y, place] = product[at : at + 8]
    out_ref[...] = scr[...].reshape(out_ref.shape).astype(bf16)


def hidden_kernel(info, terms_ref, x_ref, gain_ref, ids_ref, gates_ref, hidden_ref, packed_ref):
    attention = jnp.sum(terms_ref[...].astype(f32), axis=0)
    rounded = (x_ref[...].astype(f32) + attention).astype(bf16)
    hidden_ref[...] = rounded
    hidden = rounded.astype(f32)
    features = hidden.shape[1]
    gained = (hidden * gain_ref[...]).astype(bf16)
    columns = [ids_ref[...].astype(f32), *split3(gates_ref[...])]
    columns += split3(jnp.sum(hidden * hidden, axis=1, keepdims=True))
    extra = jnp.concatenate([*columns, jnp.zeros((hidden.shape[0], 29), f32)], axis=1)
    extra = extra.astype(bf16)
    for i in range(packed_ref.shape[0]):
        packed_ref[i, :, :features] = gained
        packed_ref[i, :, features:] = extra


def products(x_ref, w_ref):
    shards, rows, _ = x_ref.shape
    features = w_ref.shape[2]
    both = jnp.zeros((rows, 256), f32)
    tails = jnp.zeros((rows, 64), f32)
    for s in range(shards):
        x = x_ref[s]
        both += nn(x[:, :features], jnp.concatenate([w_ref[0, s], w_ref[1, s]], axis=1))
        tails += x[:, features:].astype(f32)
    return both, tails


def near_kernel(info, near_ref, w_ref, both_ref, tails_ref):
    both_ref[...], tails_ref[...] = products(near_ref, w_ref)


def expert_kernel(info, near_ref, far_ref, w_ref, both_ref, tails_ref, act_ref, place_ref, gate_ref):
    shards, features, block = w_ref.shape[1], w_ref.shape[2], 16
    both, tails = products(far_ref, w_ref)
    both = jnp.concatenate([both_ref[...], both], axis=0)
    tails = jnp.concatenate([tails_ref[...], tails], axis=0)
    rows, slots = both.shape[0], act_ref.shape[0]
    squares = tails[:, 32:33] + tails[:, 33:34] + tails[:, 34:35]
    factor = lax.rsqrt(squares * (1.0 / (shards * features)) + epsilon)
    gate = both[:, :128] * factor
    act = (gate * (1.0 / (1.0 + jnp.exp(-gate))) * (both[:, 128:] * factor)).astype(bf16)
    extra = jnp.concatenate([near_ref[0, :, features:], far_ref[0, :, features:]], axis=0).astype(f32)
    hit = extra[:, 0:8] == info[3].astype(f32)
    mask = jnp.sum(jnp.where(hit, 1.0, 0.0), axis=1, keepdims=True)
    gates = extra[:, 8:16] + extra[:, 16:24] + extra[:, 24:32]
    gate_ref[...] = jnp.sum(jnp.where(hit, gates, 0.0), axis=1, keepdims=True)
    j = lax.broadcasted_iota(jnp.int32, (rows, rows), 0)
    k = lax.broadcasted_iota(jnp.int32, (rows, rows), 1)
    before = jnp.where((k < j) & (k // block == j // block), 1.0, 0.0).astype(bf16)
    slot = nn(before, jnp.broadcast_to(mask, (rows, 128)).astype(bf16))[:, 0:1]
    j = lax.broadcasted_iota(jnp.int32, (rows, slots), 0)
    i = lax.broadcasted_iota(jnp.int32, (rows, slots), 1)
    target = slot.astype(jnp.int32) + CAP * (j // block)
    place = jnp.where((mask > 0.5) & (target == i), 1.0, 0.0).astype(bf16)
    place_ref[...] = place
    act_ref[...] = tn(place, act).astype(bf16)


def experts(info, near, far, w_in):
    slots, rows = 16 * CAP, near.shape[1]
    both, tails = call(
        near_kernel,
        [jax.ShapeDtypeStruct((rows, 256), f32), jax.ShapeDtypeStruct((rows, 64), f32)],
        [info, near, w_in],
        mib=16,
    )
    return call(
        expert_kernel,
        [
            jax.ShapeDtypeStruct((slots, 128), bf16),
            jax.ShapeDtypeStruct((2 * rows, slots), bf16),
            jax.ShapeDtypeStruct((2 * rows, 1), f32),
        ],
        [info, near, far, w_in, both, tails],
        mib=16,
    )


def cut_down_kernel(info, w_ref, o0, o1, o2, o3, held, sems):
    features = o0.shape[1]
    for place in range(SIDE):
        step = jnp.bitwise_xor(info[6], place)
        for square in range(SIDE):
            at = (NEIGHBOURS[place] + SQUARES[square]) * features
            held[step, square] = w_ref[:, at : at + features].T
    copies = [
        pltpu.make_async_copy(held.at[d], out, sems.at[d]) for d, out in enumerate((o0, o1, o2, o3))
    ]
    for copy in copies:
        copy.start()
    for copy in copies:
        copy.wait()


def cut_down(info, w_down, features):
    anywhere = pl.BlockSpec(memory_space=pltpu.HBM)
    shape = (SIDE, features, w_down.shape[0])
    return pl.pallas_call(
        cut_down_kernel,
        out_shape=[pltpu.HBM(shape, bf16)] * SIDE,
        in_specs=[SMEM, VMEM],
        out_specs=[anywhere] * SIDE,
        scratch_shapes=[
            pltpu.VMEM((SIDE,) + shape, bf16),
            pltpu.SemaphoreType.DMA((SIDE,)),
        ],
        compiler_params=pltpu.CompilerParams(vmem_limit_bytes=8 << 20),
    )(info, w_down)


def down_kernel(info, a0, a1, a2, a3, w0, w1, w2, w3, place_ref, gate_ref, near_ref, far_ref):
    place, gates = place_ref[...], gate_ref[...]
    half = near_ref.shape[1]
    for square in range(SIDE):
        total = sum(nt(a[...], w[square]) for a, w in ((a0, w0), (a1, w1), (a2, w2), (a3, w3)))
        high = total.astype(bf16)
        low = (total - high.astype(f32)).astype(bf16)
        share = (nn(place, high) + nn(place, low)) * gates
        near_ref[square] = share[:half]
        far_ref[square] = share[half:].astype(bf16)


def prompt_kernel(info, q_ref, keys_hbm, out_ref, keys_ref, scores, weighted, sems):
    pieces, tokens = keys_ref.shape[0], q_ref.shape[0]
    step, unroll = pl.program_id(0), 8

    def fetch(i):
        part = pl.ds(i * unroll, unroll)
        return pltpu.make_async_copy(keys_hbm.at[part], keys_ref.at[part], sems.at[i])

    @pl.when(step == 0)
    def _():
        for i in range(pieces // unroll):
            fetch(i).start()

    heads = q_ref.shape[1] // 576
    me, prefix_len = info[4], info[5]
    queries = jnp.concatenate([q_ref[:, h * 576 : (h + 1) * 576] for h in range(heads)], axis=0)
    rows = queries.shape[0]
    lane = lax.broadcasted_iota(jnp.int32, (tokens, 128), 1)
    ahead = lane - lax.broadcasted_iota(jnp.int32, (tokens, 128), 0)

    def score(i, top):
        @pl.when(step == 0)
        def _():
            fetch(i).wait()

        for u in range(unroll):
            j = i * unroll + u
            early = jnp.where(lane < prefix_len - j * 128, 0.0, LOW)
            late = jnp.where(ahead <= (me - j) * tokens, 0.0, LOW)
            masks = jnp.concatenate([jnp.concatenate([early, late], axis=1)] * heads, axis=0)
            s = nn(queries, keys_ref[j]) + masks
            scores[j] = s
            top = jnp.maximum(top, jnp.maximum(s[:, :128], s[:, 128:]))
        return top

    top = lax.fori_loop(0, pieces // unroll, score, jnp.full((rows, 128), LOW, f32))
    top = jnp.max(top, axis=1, keepdims=True) * score_scale
    weighted[...] = jnp.zeros_like(weighted)

    def weigh(i, total):
        sums = jnp.zeros(weighted.shape, f32)
        for u in range(unroll):
            j = i * unroll + u
            p = jnp.exp(scores[j] * score_scale - top)
            total = total + (p[:, :128] + p[:, 128:])
            sums = sums + nt(p.astype(bf16), keys_ref[j, :LATENT])
        weighted[...] += sums
        return total

    total = lax.fori_loop(0, pieces // unroll, weigh, jnp.zeros((rows, 128), f32))
    total = jnp.sum(total, axis=1, keepdims=True)
    result = (weighted[...] / total).astype(bf16)
    for h in range(heads):
        out_ref[:, h * LATENT : (h + 1) * LATENT] = result[h * tokens : (h + 1) * tokens]

def prompt_attention(info, queries, keys, heads=4):
    tokens, width = queries.shape
    steps = width // (576 * heads)
    pieces = keys.shape[0]
    hbm = pl.BlockSpec(memory_space=pltpu.HBM)
    return pl.pallas_call(
        prompt_kernel,
        out_shape=jax.ShapeDtypeStruct((tokens, steps * heads * LATENT), bf16),
        grid=(steps,),
        in_specs=[SMEM, pl.BlockSpec((tokens, heads * 576), lambda i: (0, i)), hbm],
        out_specs=pl.BlockSpec((tokens, heads * LATENT), lambda i: (0, i)),
        scratch_shapes=[
            pltpu.VMEM(keys.shape, bf16),
            pltpu.VMEM((pieces, heads * tokens, 256), f32),
            pltpu.VMEM((heads * tokens, LATENT), f32),
            pltpu.SemaphoreType.DMA((pieces // 8,)),
        ],
        compiler_params=pltpu.CompilerParams(vmem_limit_bytes=32 << 20),
        cost_estimate=pl.CostEstimate(
            flops=2 * 8 * tokens * 4096 * 1088, bytes_accessed=8 << 20, transcendentals=8 * tokens * 4096
        ),
    )(info, in_hbm(queries), in_hbm(keys))


def on_device(
    q_pre,
    prefix_cache,
    span_cache,
    prefix_len,
    q_dec,
    dec_cache,
    cache_len,
    requests,
    w_uv,
    w_out,
    x_dec,
    norm_gain,
    expert_ids,
    expert_gates,
    w_in,
    w_down,
):
    group = lax.axis_index("group")
    seq = lax.axis_index("seq")
    z = lax.axis_index("expert")
    shards = lax.axis_size("seq")
    depth = lax.axis_size("expert")
    info = jnp.stack(
        [
            group,
            seq // SIDE,
            seq % SIDE,
            group * depth + z,
            seq,
            prefix_len[0],
            seq % 2 + seq // SIDE % 2 * 2,
            seq // 2 % 2 + seq // (2 * SIDE) * 2,
        ]
    ).astype(jnp.int32)
    features = x_dec.shape[1]

    wanted = jnp.broadcast_to(requests.astype(bf16)[:, None], (8, 128))
    packet = jnp.concatenate(
        [
            jnp.concatenate([q_dec[:, : 4 * 576], wanted], axis=1),
            jnp.concatenate([q_dec[:, 4 * 576 :], wanted], axis=1),
        ],
        axis=0,
    )
    span, packet, prefix, columns = lax.optimization_barrier(
        (span_cache[0], packet, prefix_cache[0], span_cache[0])
    )
    keys = lax.all_gather(jnp.concatenate([prefix, columns], axis=1), "seq", axis=0)
    pieces, packets = along_x(span), along_y(packet)
    pieces, packets = lax.optimization_barrier((pieces, packets))
    resident = resident_attention(cache_len, packets[0], dec_cache)
    stacked = stack_of(pieces)
    part = call(
        span_kernel,
        jax.ShapeDtypeStruct((32, 9 * VDIM), bf16),
        [info, *[in_vmem(v) for v in (*packets, stacked, other_core(stacked))], w_uv, in_vmem(resident)],
        [pltpu.VMEM((SIDE, 8, 9 * VDIM), f32)],
        fetch=(7,),
        mib=16,
    )
    part, w_back = lax.optimization_barrier((part, w_down[0]))
    parts = along_y(part)
    w_back = cut_down(info, w_back, features)
    parts, w_back = lax.optimization_barrier((parts, w_back))
    *w_back, diagonal = [w_back[0]] + [swap(w_back[d], NEIGHBOURS[d]) for d in (1, 2)] + [w_back[3]]
    dec_val = call(
        merge_kernel,
        jax.ShapeDtypeStruct((32, 8 * VDIM), bf16),
        [info, *parts],
    )
    values = along_x(dec_val)
    product = call(
        project_kernel,
        jax.ShapeDtypeStruct((128, features), bf16),
        [info, *values, w_out.T],
        [pltpu.VMEM((SIDE, SIDE, 8, features), f32)],
    )
    product, expert_ids, expert_gates, norm_gain, x_dec = lax.optimization_barrier(
        (product, expert_ids, expert_gates, norm_gain, x_dec)
    )
    terms = lax.all_to_all(product.reshape(depth, 16, features), "expert", 0, 0, tiled=True)

    gain = lax.dynamic_slice(norm_gain, (seq * features,), (features,))[None]
    hidden, packed = call(
        hidden_kernel,
        [
            jax.ShapeDtypeStruct((16, features), bf16),
            jax.ShapeDtypeStruct((depth, 16, features + 64), bf16),
        ],
        [info, terms, x_dec, gain, expert_ids, expert_gates],
    )
    rows = lax.all_to_all(packed, "expert", 0, 0, tiled=True).reshape(16 * depth, features + 64)
    rows, q_pre, w_back = lax.optimization_barrier((rows, q_pre, w_back))
    arrived = everyone(rows, "seq", shards)
    o_pre = prompt_attention(info, q_pre[0], keys)
    arrived, o_pre, diagonal = lax.optimization_barrier((arrived, o_pre, diagonal))
    w_back.append(swap(diagonal, NEIGHBOURS[3]))
    act, place, gate = experts(
        info, arrived, other_core(arrived), w_in[0].reshape(2, shards, features, 128)
    )
    shape = (SIDE, 16 * depth, features)
    near, far_share = call(
        down_kernel,
        [jax.ShapeDtypeStruct(shape, f32), jax.ShapeDtypeStruct(shape, bf16)],
        [info, act, *[swap(act, mask) for mask in NEIGHBOURS[1:]], *w_back, place, gate],
        mib=16,
    )
    share = (near + other_core(far_share).astype(f32)).astype(bf16)
    same_place = [[place + square for square in SQUARES] for place in NEIGHBOURS]
    parts = lax.all_to_all(share, "seq", 0, 0, tiled=True, axis_index_groups=same_place)
    share = jnp.sum(parts.astype(f32), axis=0).astype(bf16)
    shares = lax.all_to_all(share.reshape(depth, 16, features), "expert", 0, 0, tiled=True)
    h_out = (hidden.astype(f32) + jnp.sum(shares.astype(f32), axis=0)).astype(bf16)

    return (o_pre[None], h_out)


def solution(mesh):
    return jax.shard_map(
        on_device,
        mesh=mesh,
        in_specs=(
            P("group", "seq", "expert"),
            P("group", None, "seq"),
            P("group", None, "seq"),
            P("group"),
            P(("group", "seq"), "expert"),
            P(("group", "seq"), None, None),
            P(("group", "seq")),
            P(("group", "seq")),
            P("expert", None, None),
            P("expert", "seq"),
            P(("group", "expert"), "seq"),
            P(),
            P(("group", "expert"), None),
            P(("group", "expert"), None),
            P(("group", "expert"), None, None, "seq"),
            P(("group", "expert"), "seq", None),
        ),
        out_specs=(P("group", "seq", "expert"), P(("group", "expert"), "seq")),
        check_vma=False,
    )
```
